32 devices in a mesh: row: 4 (over x, core), col: 8 (over z, y).
Axes of the slice: x: 2, y: 2, z: 4, core: 2. Of those that a mesh axis runs over, the one named last changes fastest.
Arguments:
- alignment: bfloat16 [32, 64, 256], P(None, ('row', 'col')), may hold values from -60 to 60
- norm_gain: float32 [256], replicated, may hold values from 0.1 to 1.9
- norm_bias: float32 [256], replicated, may hold values from -3 to 3
- proj_weight: bfloat16 [256, 64], replicated, may hold values from -0.375 to 0.375
- pair_weight: bfloat16 [1024, 128], replicated, may hold values from -1 to 1
- pair_bias: float32 [128], replicated, may hold values from -3 to 3
- head_weight: bfloat16 [128, 64], replicated, may hold values from -24 to 24
- head_bias: float32 [64], replicated, may hold values from -6 to 6
- labels: int32 [64, 64], P('row', 'col'), may hold values from 0 to 63, as said below
- pair_mask: int32 [64, 64], P('row', 'col'), may hold values from 0 to 1, as said below
- loss_scale: float32 [], replicated, may hold values from 256 to 1024
Outputs:
- distogram_loss: float32 [], replicated
- alignment_grad: float32 [32, 64, 256], P(None, ('row', 'col'))
- pair_weight_grad: float32 [1024, 128], replicated
The draws below stay inside these ranges and needn't reach their ends.
Inputs may be any that keep to these rules, and one draw needn't show every extreme that they name: labels is symmetric, labels[i, i] = 0, and labels[0, 63] = labels[63, 0] = 63. pair_mask[i, j] = v[i] * v[j] for a 0/1 vector v over the residues, with v[0] = 1 and v[63] = 0.
All inputs are finite; a program needn't handle non-finite values.
Results may differ from the reference program's by a relative error of at most 0.0064.
Values may be sent and summed in bfloat16 or wider, within the bound.
No kernel may reach another device: no remote copies, remote signals or barrier semaphores. Data moves between devices by JAX's collectives and lax.ppermute only.
A program may use at most 64 MiB of HBM per device.

```python
import math
import jax
import jax.numpy as jnp
from jax import lax

CM = 256
CO = 32
CZ = 128
BINS = 64
S = 32
RES_COL = 8
R = 64


def draw_alignment(key, part):
    key = jax.random.fold_in(key, 11)
    keys = jax.random.split(key, 3)
    row_scale = jnp.exp(jax.random.uniform(keys[0], (S, R, 1), minval=jnp.log(0.3), maxval=jnp.log(3.0)))
    channel_scale = jnp.exp(jax.random.uniform(keys[1], (1, 1, CM), minval=jnp.log(0.3), maxval=jnp.log(3.0)))
    noise = jax.random.normal(keys[2], (S, R, CM))
    return jnp.clip(noise * row_scale * channel_scale, -60.0, 60.0).astype(jnp.bfloat16)


def draw_head_weight(key, part):
    key = jax.random.fold_in(key, 23)
    keys = jax.random.split(key, 1)
    base = jax.random.normal(keys[0], (CZ, BINS))
    weight = base * (2.0 * CZ ** (-0.5))
    return jnp.clip(weight, -24.0, 24.0).astype(jnp.bfloat16)


def draw_labels(key, part):
    key = jax.random.fold_in(key, 31)
    raw = jax.random.randint(key, (R, R), 0, BINS // 2 + 1)
    rows = lax.broadcasted_iota(jnp.int32, (R, R), 0)
    cols = lax.broadcasted_iota(jnp.int32, (R, R), 1)
    noise = jnp.where(rows <= cols, raw, raw.T)
    base = jnp.abs(rows - cols) * (BINS // 2) // R
    binned = jnp.where(rows == cols, 0, base + noise)
    corner = (rows == 0) & (cols == R - 1) | (rows == R - 1) & (cols == 0)
    return jnp.where(corner, BINS - 1, binned).astype(jnp.int32)


def draw_pair_mask(key, part):
    key = jax.random.fold_in(key, 47)
    ticket = jax.random.randint(key, (R,), 0, 100)
    position = jnp.arange(R, dtype=jnp.int32)
    valid = ((ticket < 30 + 65 * position // R) | (position == 0)) & (position != R - 1)
    vector = valid.astype(jnp.int32)
    return (vector[:, None] * vector[None, :]).astype(jnp.int32)


def normal_values(rng, shape, scale, most, kind=jnp.bfloat16):
    entries = jax.random.normal(rng, shape, jnp.float32) * scale
    return jnp.minimum(jnp.maximum(entries, -most), most).astype(kind)


def setup_inputs(seed: int = 0) -> dict:
    streams_of = jax.random.split(jax.random.key(seed), 12)
    alignment = draw_alignment(jax.random.fold_in(streams_of[11], 71), 0)
    norm_gain = jnp.clip(1.0 + 0.18 * jax.random.normal(streams_of[1], (CM,), jnp.float32), 0.1, 1.9)
    norm_bias = normal_values(streams_of[2], (CM,), 0.5, 3.0, jnp.float32)
    proj_weight = normal_values(streams_of[3], (CM, 2 * CO), CM ** -0.5, 0.375)
    pair_weight = normal_values(streams_of[4], (CO * CO, CZ), (CO * CO // S) ** -0.5, 1.0)
    pair_bias = normal_values(streams_of[5], (CZ,), 0.5, 3.0, jnp.float32)
    head_weight = draw_head_weight(jax.random.fold_in(streams_of[11], 71), 0)
    head_bias = normal_values(streams_of[7], (BINS,), 1.0, 6.0, jnp.float32)
    labels = draw_labels(jax.random.fold_in(streams_of[11], 71), 0)
    pair_mask = draw_pair_mask(jax.random.fold_in(streams_of[11], 71), 0)
    loss_scale = jnp.clip(jnp.exp(jax.random.uniform(streams_of[10], (), jnp.float32, math.log(256.0), math.log(1024.0))), 256.0, 1024.0)
    return dict(alignment=alignment, norm_gain=norm_gain, norm_bias=norm_bias, proj_weight=proj_weight, pair_weight=pair_weight, pair_bias=pair_bias, head_weight=head_weight, head_bias=head_bias, labels=labels, pair_mask=pair_mask, loss_scale=loss_scale)


norm_eps = 1e-05
highest = lax.Precision.HIGHEST

def normalize(alignment, norm_gain, norm_bias):
    values = alignment.astype(jnp.float32)
    centered = values - lax.optimization_barrier(jnp.mean(values, axis=-1, keepdims=True))
    inverse = lax.rsqrt(lax.optimization_barrier(jnp.mean(centered * centered, axis=-1, keepdims=True)) + norm_eps)
    scaled = centered * inverse
    normed = lax.optimization_barrier((scaled * norm_gain + norm_bias).astype(jnp.bfloat16))
    return (scaled, inverse, normed)

def outer_block(left_proj, right_proj):
    outer = jnp.einsum('sic,sjd->ijcd', left_proj.astype(jnp.float32), right_proj.astype(jnp.float32))
    outer = outer * (1.0 / left_proj.shape[0])
    rounded = lax.optimization_barrier(outer.astype(jnp.bfloat16))
    return rounded.reshape(-1, outer.shape[2] * outer.shape[3])

def reference(alignment, norm_gain, norm_bias, proj_weight, pair_weight, pair_bias, head_weight, head_bias, labels, pair_mask, loss_scale):
    scaled, inverse, normed = normalize(alignment, norm_gain, norm_bias)
    projected = jnp.einsum('src,cp->srp', normed.astype(jnp.float32), proj_weight.astype(jnp.float32))
    projected = lax.optimization_barrier(projected.astype(jnp.bfloat16))
    left_all = projected[:, :, :CO]
    right_all = projected[:, :, CO:]
    pair32 = pair_weight.astype(jnp.float32)
    head32 = head_weight.astype(jnp.float32)
    starts = jnp.arange(R // RES_COL, dtype=jnp.int32) * RES_COL

    def forward(first_row):
        left_proj = lax.dynamic_slice_in_dim(left_all, first_row, RES_COL, 1)
        features = outer_block(left_proj, right_all)
        hidden = jnp.dot(features, pair_weight, preferred_element_type=jnp.float32) + pair_bias
        return (jnp.dot(hidden, head32, precision=highest) + head_bias).reshape(RES_COL, R, BINS)
    half_logits = lax.map(forward, starts).reshape(R, R, BINS)
    logits = half_logits + jnp.transpose(half_logits, (1, 0, 2))
    row_top = lax.optimization_barrier(jnp.max(logits, axis=-1, keepdims=True))
    shifted = logits - row_top
    exp_shift = jnp.exp(shifted)
    exp_total = lax.optimization_barrier(jnp.sum(exp_shift, axis=-1, keepdims=True))
    bins_iota = lax.broadcasted_iota(jnp.int32, logits.shape, 2)
    target = bins_iota == labels[:, :, None]
    picked = lax.optimization_barrier(jnp.sum(jnp.where(target, shifted, 0.0), axis=-1))
    mask_values = pair_mask.astype(jnp.float32)
    valid_pairs = jnp.sum(mask_values)
    distogram_loss = jnp.sum(mask_values * (jnp.log(exp_total[:, :, 0]) - picked)) / valid_pairs
    dlogits = (exp_shift / exp_total - target.astype(jnp.float32)) * (mask_values * (loss_scale / valid_pairs))[:, :, None]
    dlogits = lax.optimization_barrier(dlogits.astype(jnp.bfloat16)).astype(jnp.float32)
    dhalf = dlogits + jnp.transpose(dlogits, (1, 0, 2))

    def backward(carry, first_row):
        weight_sum, right_grad = carry
        left_proj = lax.dynamic_slice_in_dim(left_all, first_row, RES_COL, 1)
        features = outer_block(left_proj, right_all)
        dhalf_rows = lax.dynamic_slice_in_dim(dhalf, first_row, RES_COL, 0).reshape(-1, BINS)
        dhidden = jnp.dot(dhalf_rows, head32.T, precision=highest)
        dfeatures = jnp.dot(dhidden, pair32.T, precision=highest)
        dfeatures = lax.optimization_barrier(dfeatures.astype(jnp.bfloat16)).astype(jnp.float32)
        dfeatures = dfeatures.reshape(RES_COL, R, CO, CO)
        weight_sum = weight_sum + jnp.dot(features.astype(jnp.float32).T, dhidden, precision=highest)
        left_grad = jnp.einsum('ijcd,sjd->sic', dfeatures, right_all.astype(jnp.float32)) * (1.0 / S)
        right_grad = right_grad + jnp.einsum('ijcd,sic->sjd', dfeatures, left_proj.astype(jnp.float32)) * (1.0 / S)
        return ((weight_sum, right_grad), left_grad)
    initial = (jnp.zeros((CO * CO, CZ), jnp.float32), jnp.zeros((S, R, CO), jnp.float32))
    (pair_weight_grad, right_grad), left_blocks = lax.scan(backward, initial, starts)
    left_grad = jnp.transpose(left_blocks, (1, 0, 2, 3)).reshape(S, R, CO)
    projected_grad = jnp.concatenate([left_grad, right_grad], axis=-1)
    dnormed = jnp.einsum('srp,cp->src', projected_grad, proj_weight.astype(jnp.float32), precision=highest)
    dscaled = dnormed * norm_gain
    alignment_grad = inverse * (dscaled - lax.optimization_barrier(jnp.mean(dscaled, axis=-1, keepdims=True)) - scaled * lax.optimization_barrier(jnp.mean(dscaled * scaled, axis=-1, keepdims=True)))
    return (distogram_loss, alignment_grad, pair_weight_grad)
```

```python
import functools

import jax
import jax.numpy as jnp
from jax import lax
from jax.experimental import pallas as pl
from jax.experimental.pallas import tpu as pltpu
from jax.sharding import PartitionSpec as P

norm_eps = 1e-05
highest = lax.Precision.HIGHEST


def from_root(value, axis, source):
    kept = jnp.where(lax.axis_index(axis) == source, value, 0).astype(value.dtype)
    return lax.psum(kept, axis)


def normalize(alignment, norm_gain, norm_bias):
    values = alignment.astype(jnp.float32)
    centered = values - jnp.mean(values, axis=-1, keepdims=True)
    inverse = lax.rsqrt(jnp.mean(centered * centered, axis=-1, keepdims=True) + norm_eps)
    scaled = centered * inverse
    normed = (scaled * norm_gain + norm_bias).astype(jnp.bfloat16)
    return (scaled, inverse, normed)


def pair_features(left_proj, right_proj, mirrored):
    if mirrored:
        outer = jnp.einsum(
            "sid,sjc->ijcd", left_proj, right_proj, preferred_element_type=jnp.float32
        )
    else:
        outer = jnp.einsum(
            "sic,sjd->ijcd", left_proj, right_proj, preferred_element_type=jnp.float32
        )
    outer = outer * (1.0 / left_proj.shape[0])
    return outer.astype(jnp.bfloat16).reshape(-1, outer.shape[2] * outer.shape[3])


def local(
    alignment,
    norm_gain,
    norm_bias,
    proj_weight,
    pair_weight,
    pair_bias,
    head_weight,
    head_bias,
    labels,
    pair_mask,
    loss_scale,
):
    per_row = lax.axis_size("col") // lax.axis_size("row")
    col_place = lax.axis_index("col")
    row_place = lax.axis_index("row")
    sequences = alignment.shape[0]
    outer_width = proj_weight.shape[1] // 2
    bin_count = head_weight.shape[1]
    scaled, inverse, normed = normalize(alignment, norm_gain, norm_bias)
    projected = jnp.einsum(
        "src,cp->srp", normed, proj_weight, preferred_element_type=jnp.float32
    ).astype(jnp.bfloat16)
    mask_values = pair_mask.astype(jnp.float32)
    valid_pairs = lax.psum(jnp.sum(mask_values), ("row", "col"))
    row_proj = lax.all_gather(projected, "col", axis=1, tiled=True)
    row_span = row_proj.shape[1]
    col_span = row_span // per_row
    offset = col_place % per_row * col_span
    own_slice = lax.dynamic_slice_in_dim(row_proj, offset, col_span, 1)
    col_proj = from_root(own_slice, "row", col_place // per_row)
    pair32 = pair_weight.astype(jnp.float32)
    head32 = head_weight.astype(jnp.float32)
    weight_shape = pair32.shape
    grad_width = 2 * outer_width
    block_rows = min(row_span, max(1, 512 // col_span))
    num_blocks = row_span // block_rows
    grad_factor = loss_scale / valid_pairs
    inv_seqs = 1.0 / sequences
    bins_iota = lax.broadcasted_iota(jnp.int32, (block_rows * col_span, bin_count), 1)

    def pair_head(features):
        hidden = jnp.dot(features, pair_weight, preferred_element_type=jnp.float32) + pair_bias
        return jnp.dot(hidden, head32, precision=highest) + head_bias

    def tile_back(features, dhalf, left_proj, right_proj, mirrored):
        dhidden = jnp.dot(dhalf, head_weight.T, preferred_element_type=jnp.float32)
        dfeatures = jnp.dot(dhidden, pair32.T, precision=highest)
        weight_term = jnp.dot(features.astype(jnp.float32).T, dhidden, precision=highest)
        dfeatures = dfeatures.astype(jnp.bfloat16).reshape(
            left_proj.shape[1], right_proj.shape[1], outer_width, outer_width
        )
        if mirrored:
            grad_left = jnp.einsum(
                "ijcd,sjc->sid", dfeatures, right_proj, preferred_element_type=jnp.float32
            )
            grad_right = jnp.einsum(
                "ijcd,sid->sjc", dfeatures, left_proj, preferred_element_type=jnp.float32
            )
        else:
            grad_left = jnp.einsum(
                "ijcd,sjd->sic", dfeatures, right_proj, preferred_element_type=jnp.float32
            )
            grad_right = jnp.einsum(
                "ijcd,sic->sjd", dfeatures, left_proj, preferred_element_type=jnp.float32
            )
        return (grad_left * inv_seqs, grad_right * inv_seqs, weight_term)

    def block_step(block_index, carry):
        loss_sum, weight_sum, row_grad, col_grad = carry
        first_row = block_index * block_rows
        rows_here = lax.dynamic_slice_in_dim(row_proj, first_row, block_rows, 1)
        left_own = rows_here[:, :, :outer_width]
        left_mirror = rows_here[:, :, outer_width:]
        right_own = col_proj[:, :, outer_width:]
        right_mirror = col_proj[:, :, :outer_width]
        own_features = pair_features(left_own, right_own, False)
        mirror_features = pair_features(left_mirror, right_mirror, True)
        logits = pair_head(own_features) + pair_head(mirror_features)
        labels_here = lax.dynamic_slice_in_dim(labels, first_row, block_rows, 0).reshape(-1)
        mask_here = lax.dynamic_slice_in_dim(mask_values, first_row, block_rows, 0).reshape(-1)
        row_top = jnp.max(logits, axis=-1, keepdims=True)
        shifted = logits - row_top
        exp_shift = jnp.exp(shifted)
        exp_total = jnp.sum(exp_shift, axis=-1, keepdims=True)
        target = bins_iota == labels_here[:, None]
        picked = jnp.sum(jnp.where(target, shifted, 0.0), axis=-1)
        loss_sum = loss_sum + jnp.sum(mask_here * (jnp.log(exp_total[:, 0]) - picked))
        dlogits = (
            (exp_shift / exp_total - target.astype(jnp.float32))
            * (mask_here * grad_factor)[:, None]
        ).astype(jnp.bfloat16)
        grad_left, grad_right, weight_term = tile_back(
            own_features, dlogits, left_own, right_own, False
        )
        mirror_left, mirror_right, mirror_term = tile_back(
            mirror_features, dlogits, left_mirror, right_mirror, True
        )
        row_part = jnp.concatenate([grad_left, mirror_left], axis=-1)
        col_part = jnp.concatenate([mirror_right, grad_right], axis=-1)
        weight_term = weight_term + mirror_term
        row_grad = lax.dynamic_update_slice_in_dim(row_grad, row_part, first_row, 1)
        return (loss_sum, weight_sum + weight_term, row_grad, col_grad + col_part)

    initial = (
        jnp.zeros((), jnp.float32),
        jnp.zeros(weight_shape, jnp.float32),
        jnp.zeros((sequences, row_span, grad_width), jnp.float32),
        jnp.zeros((sequences, col_span, grad_width), jnp.float32),
    )
    loss_sum, weight_sum, row_grad, col_grad = lax.fori_loop(0, num_blocks, block_step, initial)
    holder = col_place // per_row == row_place
    col_sum = lax.psum(col_grad.astype(jnp.bfloat16), "row").astype(jnp.float32)
    placed = lax.dynamic_update_slice_in_dim(jnp.zeros_like(row_grad), col_sum, offset, 1)
    contribution = row_grad + jnp.where(holder, placed, 0.0)
    own_grad = lax.psum_scatter(contribution, "col", scatter_dimension=1, tiled=True)
    dnormed = jnp.einsum(
        "srp,cp->src", own_grad, proj_weight.astype(jnp.float32), precision=highest
    )
    dscaled = dnormed * norm_gain
    alignment_grad = inverse * (
        dscaled
        - jnp.mean(dscaled, axis=-1, keepdims=True)
        - scaled * jnp.mean(dscaled * scaled, axis=-1, keepdims=True)
    )
    loss_total, pair_weight_grad = lax.psum((loss_sum, weight_sum), ("row", "col"))
    return (loss_total / valid_pairs, alignment_grad, pair_weight_grad)


f32 = jnp.float32
bf16 = jnp.bfloat16
NN = (((1,), (0,)), ((), ()))
NT = (((1,), (1,)), ((), ()))


def dot(a, b, dims=NN):
    return lax.dot_general(a, b, dims, preferred_element_type=f32)


def layer_norm(x):
    centered = x - jnp.mean(x, axis=-1, keepdims=True)
    inverse = lax.rsqrt(jnp.mean(centered * centered, axis=-1, keepdims=True) + norm_eps)
    return centered * inverse, inverse


def prepare_kernel(align_ref, gain_ref, bias_ref, weight_ref, labels_ref, mask_ref, out_ref):
    align = align_ref[...].astype(f32)
    weight = weight_ref[...]
    plain = []
    for r in range(2):
        scaled, _ = layer_norm(align[:, r, :])
        normed = (scaled * gain_ref[...] + bias_ref[...]).astype(bf16)
        turned = dot(weight, normed, NT)
        rows = [
            jnp.concatenate([turned[h * 32 + q * 8 : h * 32 + q * 8 + 8] for q in range(4)], axis=1)
            for h in range(2)
        ]
        out_ref[r * 16 : r * 16 + 16, :] = jnp.concatenate(rows, axis=0).astype(bf16)
        plain.append(dot(normed, weight[32:64], NT))
    out_ref[32:48, :] = jnp.concatenate(
        [plain[r][h * 16 : h * 16 + 16] for h in range(2) for r in range(2)], axis=1
    ).astype(bf16)
    lane = lax.broadcasted_iota(jnp.int32, (16, 128), 1)
    spread = (lane // 8 == lax.broadcasted_iota(jnp.int32, (16, 128), 0)).astype(bf16)
    keep = lane[:8] % 8 == lax.broadcasted_iota(jnp.int32, (8, 128), 0)
    flat = []
    for ref in (labels_ref, mask_ref):
        wide = dot(ref[...].astype(f32).astype(bf16), spread)
        flat.append(jnp.sum(jnp.where(keep, wide, 0.0), axis=0, keepdims=True))
    row = lax.broadcasted_iota(jnp.int32, (16, 128), 0)
    out_ref[48:64, :] = jnp.where(row == 0, flat[0], jnp.where(row == 1, flat[1], 0.0)).astype(bf16)


def pairs_kernel(
    place_ref, scale_ref, gathered_ref, align_ref, gain_ref, proj_ref, pair_ref, pair_bias_ref,
    head_ref, head_bias_ref, loss_ref, align_grad_ref, weight_grad_ref,
    turned_ref, left_ref, wide_ref, pair_blocks_ref, pair32_ref, features_ref, hidden_ref, dhidden_ref,
):
    turned_ref[...] = gathered_ref[:, 0:32, :].reshape(1024, 128).astype(f32)
    groups = [turned_ref[pl.ds(g, 64, stride=16), :].astype(bf16) for g in range(16)]
    for g in range(8):
        left_ref[g * 64 : g * 64 + 64, :] = groups[g]
    source = lax.broadcasted_iota(jnp.int32, (128, 512), 0)
    target = lax.broadcasted_iota(jnp.int32, (128, 512), 1)
    copies = jnp.where(source == target // 128 * 32 + target % 32, 1.0 / 32.0, 0.0).astype(bf16)
    wide_ref[...] = dot(gathered_ref[:, 32:48, :].reshape(512, 128), copies).astype(bf16)
    for g in range(8):
        for q in range(4):
            at = (q * 8 + g) * 32
            pair_blocks_ref[g * 128 + q * 32 : g * 128 + q * 32 + 32, :] = pair_ref[at : at + 32, :]
    pair32_ref[...] = pair_ref[...].astype(f32)

    lane = lax.broadcasted_iota(jnp.int32, (32, 128), 1) // 32

    def forward(d, _):
        top = pl.multiple_of(d * 16, 16)
        sides = []
        for r in range(2):
            right = jnp.concatenate(
                [wide_ref[pl.ds(top, 16), (h * 2 + r) * 128 : (h * 2 + r + 1) * 128] for h in range(2)], axis=0
            )
            sides.append(
                jnp.concatenate([jnp.where(lane == q, right, jnp.zeros_like(right)) for q in range(4)], axis=0)
            )
        outer = dot(left_ref[...], jnp.concatenate(sides, axis=1)).astype(bf16)
        first = pl.multiple_of(d * 128, 128)
        features = jnp.concatenate(
            [
                jnp.concatenate([outer[g * 64 : g * 64 + 64, r * 128 : r * 128 + 128] for g in range(8)], axis=1)
                for r in range(2)
            ],
            axis=0,
        )
        features_ref[pl.ds(first, 128), :] = features
        hidden_ref[pl.ds(first, 128), :] = dot(features, pair_blocks_ref[...]) + pair_bias_ref[...]
        return 0

    lax.fori_loop(0, 32, forward, 0, unroll=2)

    source = lax.broadcasted_iota(jnp.int32, (128, 1024), 0)
    target = lax.broadcasted_iota(jnp.int32, (128, 1024), 1)
    spread = (source == target // 64 * 8 + target % 8).astype(bf16)
    keep = (
        lax.broadcasted_iota(jnp.int32, (32, 1024), 1) // 8 % 8
        == lax.broadcasted_iota(jnp.int32, (32, 1024), 0) % 8
    )
    turned_ref[0:512, :] = gathered_ref[:, 48:64, :].reshape(512, 128).astype(f32)

    def blocks(row):
        placed = dot(turned_ref[pl.ds(row, 32, stride=16), :].astype(bf16), spread)
        return jnp.sum(jnp.where(keep, placed, 0.0).reshape(4, 8, 1024), axis=1)

    labels = blocks(0).astype(jnp.int32)
    mask = blocks(1)
    valid = jnp.sum(mask, keepdims=True)
    factor = mask * (scale_ref[0] / valid)
    head_t = head_ref[...]
    head_twice = jnp.concatenate([head_t, head_t], axis=1)
    head2 = (2.0 * head_t.astype(f32).T).astype(bf16)
    head_bias2 = 2.0 * head_bias_ref[...]
    bins = lax.broadcasted_iota(jnp.int32, (64, 256), 0)
    loss = jnp.zeros((1, 256), f32)
    for k in range(16):
        both = jnp.concatenate(
            [
                hidden_ref[j * 64 : j * 64 + 64, :] + hidden_ref[pl.ds(j, 64, stride=64), :]
                for j in range(k * 4, k * 4 + 4)
            ],
            axis=0,
        )
        high = both.astype(bf16)
        low = (both - high.astype(f32)).astype(bf16)
        logits = dot(head_twice, jnp.concatenate([high, low], axis=1), NT) + head_bias2
        part = slice(k % 4 * 256, k % 4 * 256 + 256)
        labels_here = labels[k // 4 : k // 4 + 1, part]
        shifted = logits - jnp.max(logits, axis=0, keepdims=True)
        exp_shift = jnp.exp(shifted)
        exp_total = jnp.sum(exp_shift, axis=0, keepdims=True)
        hit = bins == labels_here
        picked = jnp.sum(jnp.where(hit, shifted, 0.0), axis=0, keepdims=True)
        loss = loss + mask[k // 4 : k // 4 + 1, part] * (jnp.log(exp_total) - picked)
        dlogits = (exp_shift / exp_total - jnp.where(hit, 1.0, 0.0)) * factor[k // 4 : k // 4 + 1, part]
        dhidden_ref[:, k * 256 : k * 256 + 256] = dot(head2, dlogits.astype(bf16)).astype(bf16)
    loss_ref[...] = jnp.sum(loss, axis=1, keepdims=True) / valid

    for n in range(4):
        turned = dot(dhidden_ref[...], features_ref[:, n * 256 : n * 256 + 256]).T
        for g in range(2):
            for q in range(4):
                at = (q * 8 + n * 2 + g) * 32
                weight_grad_ref[at : at + 32, :] = turned[g * 128 + q * 32 : g * 128 + q * 32 + 32]

    place = place_ref[0]
    own = dhidden_ref[:, pl.ds(pl.multiple_of(place * 128, 128), 128)]
    own = jnp.concatenate([own[:, 0:64], own[:, 64:128]], axis=0)
    sums = dot(own, jnp.concatenate(groups, axis=1)).astype(bf16)

    def contract(weights, base):
        q_rows = jnp.concatenate(
            [
                jnp.concatenate(
                    [sums[r * 128 : r * 128 + 128, (base + g) * 128 : (base + g + 1) * 128] for r in range(2)], axis=1
                )
                for g in range(8)
            ],
            axis=0,
        )
        full = dot(jnp.concatenate(weights, axis=1), q_rows)
        row = lax.broadcasted_iota(jnp.int32, (128, 256), 0) // 32
        col = lax.broadcasted_iota(jnp.int32, (128, 256), 1) // 32 % 4
        kept = jnp.where(row == col, full, 0.0)
        return kept[0:32] + kept[32:64] + kept[64:96] + kept[96:128]

    by_left = [pair_blocks_ref[g * 128 : g * 128 + 128, :] for g in range(8)]
    by_right = [
        jnp.concatenate([pair32_ref[pl.ds(q * 8 + g, 32, stride=32), :] for q in range(4)], axis=0).astype(bf16)
        for g in range(8)
    ]
    dleft = contract(by_right, 8)
    dright = contract(by_left, 0)
    dproj = jnp.concatenate([dleft, dright], axis=0).T * (1.0 / 32.0)
    proj = proj_ref[...]
    proj_twice = jnp.concatenate([proj, proj], axis=0)
    align = align_ref[...].astype(f32)
    for r in range(2):
        at = r * 128
        one = dproj[at : at + 32] + dproj[at + 32 : at + 64] + dproj[at + 64 : at + 96] + dproj[at + 96 : at + 128]
        high = one.astype(bf16)
        low = (one - high.astype(f32)).astype(bf16)
        dscaled = dot(jnp.concatenate([high, low], axis=1), proj_twice) * gain_ref[...]
        scaled, inverse = layer_norm(align[:, r, :])
        align_grad_ref[:, r, :] = inverse * (
            dscaled
            - jnp.mean(dscaled, axis=-1, keepdims=True)
            - scaled * jnp.mean(dscaled * scaled, axis=-1, keepdims=True)
        )


def spec(space=pltpu.VMEM):
    return pl.BlockSpec(memory_space=space)


def prepare(align, gain, bias, proj_t, labels_t, mask_t):
    return pl.pallas_call(
        prepare_kernel,
        out_shape=jax.ShapeDtypeStruct((64, 128), bf16),
        in_specs=[spec()] * 6,
        out_specs=spec(),
    )(align, gain, bias, proj_t, labels_t, mask_t)


def pairs(place, scale, gathered, align, gain, proj_t, pair, pair_bias, head_t, head_bias):
    return pl.pallas_call(
        pairs_kernel,
        out_shape=(
            jax.ShapeDtypeStruct((1, 1), f32),
            jax.ShapeDtypeStruct((32, 2, 256), f32),
            jax.ShapeDtypeStruct((1024, 128), f32),
        ),
        in_specs=[spec(pltpu.SMEM)] * 2 + [spec()] * 8,
        out_specs=(spec(),) * 3,
        scratch_shapes=[
            pltpu.VMEM((1024, 128), f32),
            pltpu.VMEM((512, 128), bf16),
            pltpu.VMEM((512, 512), bf16),
            pltpu.VMEM((1024, 128), bf16),
            pltpu.VMEM((1024, 128), f32),
            pltpu.VMEM((4096, 1024), bf16),
            pltpu.VMEM((4096, 128), f32),
            pltpu.VMEM((128, 4096), bf16),
        ],
        compiler_params=pltpu.CompilerParams(vmem_limit_bytes=40 * 1024 * 1024),
    )(place, scale, gathered, align, gain, proj_t, pair, pair_bias, head_t, head_bias)


def gather(message):
    copies = jnp.broadcast_to(message[None], (32,) + message.shape)
    return lax.all_to_all(copies, ("row", "col"), 0, 0, tiled=True)


def local_whole(
    alignment, norm_gain, norm_bias, proj_weight, pair_weight, pair_bias, head_weight, head_bias,
    labels, pair_mask, loss_scale,
):
    gain = norm_gain.reshape(1, 256)
    message = prepare(alignment, gain, norm_bias.reshape(1, 256), proj_weight.T, labels.T, pair_mask.T)
    gathered = gather(message)
    place = lax.axis_index(("row", "col")).astype(jnp.int32).reshape(1)
    loss, align_grad, weight_grad = pairs(
        place, loss_scale.reshape(1), gathered, alignment, gain, proj_weight.T, pair_weight,
        pair_bias.reshape(1, 128), head_weight.T, head_bias.reshape(64, 1),
    )
    return (loss.reshape(()), align_grad, weight_grad)


def solution(mesh):
    in_specs = (
        P(None, ("row", "col"), None),
        P(),
        P(),
        P(),
        P(),
        P(),
        P(),
        P(),
        P("row", "col"),
        P("row", "col"),
        P(),
    )
    out_specs = (P(), P(None, ("row", "col"), None), P())
    def whole(alignment, *others):
        sequences, residues, channels = alignment.shape
        small = (
            (sequences, residues, channels) == (32, 64, 256)
            and tuple(mesh.shape.values()) == (4, 8)
            and others[2].shape[1] == 64
            and others[3].shape == (1024, 128)
            and others[5].shape == (128, 64)
        )
        return jax.shard_map(
            local_whole if small else local, mesh=mesh, in_specs=in_specs, out_specs=out_specs, check_vma=False
        )(alignment, *others)

    return whole
```

```python
import functools

import jax
import jax.numpy as jnp
from jax import lax
from jax.experimental import pallas as pl
from jax.experimental.pallas import tpu as pltpu
from jax.sharding import PartitionSpec as P

norm_eps = 1e-05
highest = lax.Precision.HIGHEST


def from_root(value, axis, source):
    kept = jnp.where(lax.axis_index(axis) == source, value, 0).astype(value.dtype)
    return lax.psum(kept, axis)


def normalize(alignment, norm_gain, norm_bias):
    values = alignment.astype(jnp.float32)
    centered = values - jnp.mean(values, axis=-1, keepdims=True)
    inverse = lax.rsqrt(jnp.mean(centered * centered, axis=-1, keepdims=True) + norm_eps)
    scaled = centered * inverse
    normed = (scaled * norm_gain + norm_bias).astype(jnp.bfloat16)
    return (scaled, inverse, normed)


def pair_features(left_proj, right_proj, mirrored):
    if mirrored:
        outer = jnp.einsum(
            "sid,sjc->ijcd", left_proj, right_proj, preferred_element_type=jnp.float32
        )
    else:
        outer = jnp.einsum(
            "sic,sjd->ijcd", left_proj, right_proj, preferred_element_type=jnp.float32
        )
    outer = outer * (1.0 / left_proj.shape[0])
    return outer.astype(jnp.bfloat16).reshape(-1, outer.shape[2] * outer.shape[3])


def local(
    alignment,
    norm_gain,
    norm_bias,
    proj_weight,
    pair_weight,
    pair_bias,
    head_weight,
    head_bias,
    labels,
    pair_mask,
    loss_scale,
):
    per_row = lax.axis_size("col") // lax.axis_size("row")
    col_place = lax.axis_index("col")
    row_place = lax.axis_index("row")
    sequences = alignment.shape[0]
    outer_width = proj_weight.shape[1] // 2
    bin_count = head_weight.shape[1]
    scaled, inverse, normed = normalize(alignment, norm_gain, norm_bias)
    projected = jnp.einsum(
        "src,cp->srp", normed, proj_weight, preferred_element_type=jnp.float32
    ).astype(jnp.bfloat16)
    mask_values = pair_mask.astype(jnp.float32)
    valid_pairs = lax.psum(jnp.sum(mask_values), ("row", "col"))
    row_proj = lax.all_gather(projected, "col", axis=1, tiled=True)
    row_span = row_proj.shape[1]
    col_span = row_span // per_row
    offset = col_place % per_row * col_span
    own_slice = lax.dynamic_slice_in_dim(row_proj, offset, col_span, 1)
    col_proj = from_root(own_slice, "row", col_place // per_row)
    pair32 = pair_weight.astype(jnp.float32)
    head32 = head_weight.astype(jnp.float32)
    weight_shape = pair32.shape
    grad_width = 2 * outer_width
    block_rows = min(row_span, max(1, 512 // col_span))
    num_blocks = row_span // block_rows
    grad_factor = loss_scale / valid_pairs
    inv_seqs = 1.0 / sequences
    bins_iota = lax.broadcasted_iota(jnp.int32, (block_rows * col_span, bin_count), 1)

    def pair_head(features):
        hidden = jnp.dot(features, pair_weight, preferred_element_type=jnp.float32) + pair_bias
        return jnp.dot(hidden, head32, precision=highest) + head_bias

    def tile_back(features, dhalf, left_proj, right_proj, mirrored):
        dhidden = jnp.dot(dhalf, head_weight.T, preferred_element_type=jnp.float32)
        dfeatures = jnp.dot(dhidden, pair32.T, precision=highest)
        weight_term = jnp.dot(features.astype(jnp.float32).T, dhidden, precision=highest)
        dfeatures = dfeatures.astype(jnp.bfloat16).reshape(
            left_proj.shape[1], right_proj.shape[1], outer_width, outer_width
        )
        if mirrored:
            grad_left = jnp.einsum(
                "ijcd,sjc->sid", dfeatures, right_proj, preferred_element_type=jnp.float32
            )
            grad_right = jnp.einsum(
                "ijcd,sid->sjc", dfeatures, left_proj, preferred_element_type=jnp.float32
            )
        else:
            grad_left = jnp.einsum(
                "ijcd,sjd->sic", dfeatures, right_proj, preferred_element_type=jnp.float32
            )
            grad_right = jnp.einsum(
                "ijcd,sic->sjd", dfeatures, left_proj, preferred_element_type=jnp.float32
            )
        return (grad_left * inv_seqs, grad_right * inv_seqs, weight_term)

    def block_step(block_index, carry):
        loss_sum, weight_sum, row_grad, col_grad = carry
        first_row = block_index * block_rows
        rows_here = lax.dynamic_slice_in_dim(row_proj, first_row, block_rows, 1)
        left_own = rows_here[:, :, :outer_width]
        left_mirror = rows_here[:, :, outer_width:]
        right_own = col_proj[:, :, outer_width:]
        right_mirror = col_proj[:, :, :outer_width]
        own_features = pair_features(left_own, right_own, False)
        mirror_features = pair_features(left_mirror, right_mirror, True)
        logits = pair_head(own_features) + pair_head(mirror_features)
        labels_here = lax.dynamic_slice_in_dim(labels, first_row, block_rows, 0).reshape(-1)
        mask_here = lax.dynamic_slice_in_dim(mask_values, first_row, block_rows, 0).reshape(-1)
        row_top = jnp.max(logits, axis=-1, keepdims=True)
        shifted = logits - row_top
        exp_shift = jnp.exp(shifted)
        exp_total = jnp.sum(exp_shift, axis=-1, keepdims=True)
        target = bins_iota == labels_here[:, None]
        picked = jnp.sum(jnp.where(target, shifted, 0.0), axis=-1)
        loss_sum = loss_sum + jnp.sum(mask_here * (jnp.log(exp_total[:, 0]) - picked))
        dlogits = (
            (exp_shift / exp_total - target.astype(jnp.float32))
            * (mask_here * grad_factor)[:, None]
        ).astype(jnp.bfloat16)
        grad_left, grad_right, weight_term = tile_back(
            own_features, dlogits, left_own, right_own, False
        )
        mirror_left, mirror_right, mirror_term = tile_back(
            mirror_features, dlogits, left_mirror, right_mirror, True
        )
        row_part = jnp.concatenate([grad_left, mirror_left], axis=-1)
        col_part = jnp.concatenate([mirror_right, grad_right], axis=-1)
        weight_term = weight_term + mirror_term
        row_grad = lax.dynamic_update_slice_in_dim(row_grad, row_part, first_row, 1)
        return (loss_sum, weight_sum + weight_term, row_grad, col_grad + col_part)

    initial = (
        jnp.zeros((), jnp.float32),
        jnp.zeros(weight_shape, jnp.float32),
        jnp.zeros((sequences, row_span, grad_width), jnp.float32),
        jnp.zeros((sequences, col_span, grad_width), jnp.float32),
    )
    loss_sum, weight_sum, row_grad, col_grad = lax.fori_loop(0, num_blocks, block_step, initial)
    holder = col_place // per_row == row_place
    col_sum = lax.psum(col_grad.astype(jnp.bfloat16), "row").astype(jnp.float32)
    placed = lax.dynamic_update_slice_in_dim(jnp.zeros_like(row_grad), col_sum, offset, 1)
    contribution = row_grad + jnp.where(holder, placed, 0.0)
    own_grad = lax.psum_scatter(contribution, "col", scatter_dimension=1, tiled=True)
    dnormed = jnp.einsum(
        "srp,cp->src", own_grad, proj_weight.astype(jnp.float32), precision=highest
    )
    dscaled = dnormed * norm_gain
    alignment_grad = inverse * (
        dscaled
        - jnp.mean(dscaled, axis=-1, keepdims=True)
        - scaled * jnp.mean(dscaled * scaled, axis=-1, keepdims=True)
    )
    loss_total, pair_weight_grad = lax.psum((loss_sum, weight_sum), ("row", "col"))
    return (loss_total / valid_pairs, alignment_grad, pair_weight_grad)


f32 = jnp.float32
bf16 = jnp.bfloat16
NN = (((1,), (0,)), ((), ()))
NT = (((1,), (1,)), ((), ()))


def dot(a, b, dims=NN):
    return lax.dot_general(a, b, dims, preferred_element_type=f32)


def layer_norm(x):
    centered = x - jnp.mean(x, axis=-1, keepdims=True)
    inverse = lax.rsqrt(jnp.mean(centered * centered, axis=-1, keepdims=True) + norm_eps)
    return centered * inverse, inverse


def fetch(sources, targets, sems):
    copies = [
        pltpu.make_async_copy(source, target, sems.at[n])
        for n, (source, target) in enumerate(zip(sources, targets, strict=True))
    ]
    for copy in copies:
        copy.start()
    return copies


def prepare_kernel(*refs):
    out_ref = refs[6]
    for copy in fetch(refs[:6], refs[7:13], refs[13]):
        copy.wait()
    align_ref, gain_ref, bias_ref, weight_ref, labels_ref, mask_ref = refs[7:13]
    align = align_ref[...].astype(f32)
    weight = weight_ref[...]
    plain = []
    for r in range(2):
        scaled, _ = layer_norm(align[:, r, :])
        normed = (scaled * gain_ref[...] + bias_ref[...]).astype(bf16)
        turned = dot(weight, normed, NT)
        rows = [
            jnp.concatenate([turned[h * 32 + q * 8 : h * 32 + q * 8 + 8] for q in range(4)], axis=1)
            for h in range(2)
        ]
        out_ref[r * 16 : r * 16 + 16, :] = jnp.concatenate(rows, axis=0).astype(bf16)
        plain.append(dot(normed, weight[32:64], NT))
    out_ref[32:48, :] = jnp.concatenate(
        [plain[r][h * 16 : h * 16 + 16] for h in range(2) for r in range(2)], axis=1
    ).astype(bf16)
    lane = lax.broadcasted_iota(jnp.int32, (16, 128), 1)
    spread = (lane // 8 == lax.broadcasted_iota(jnp.int32, (16, 128), 0)).astype(bf16)
    keep = lane[:8] % 8 == lax.broadcasted_iota(jnp.int32, (8, 128), 0)
    flat = []
    for ref in (labels_ref, mask_ref):
        wide = dot(ref[...].astype(f32).astype(bf16), spread)
        flat.append(jnp.sum(jnp.where(keep, wide, 0.0), axis=0, keepdims=True))
    row = lax.broadcasted_iota(jnp.int32, (16, 128), 0)
    out_ref[48:64, :] = jnp.where(row == 0, flat[0], jnp.where(row == 1, flat[1], 0.0)).astype(bf16)


def arrange_weights(pair_ref, pair_bias, head_t, head_bias, folded_ref, by_left_ref, by_right_ref, pair32_ref):
    pair32_ref[...] = pair_ref[...].astype(f32)
    head_twice = jnp.concatenate([head_t, head_t], axis=0)
    lane = lax.broadcasted_iota(jnp.int32, (128, 128), 1)
    for g in range(8):
        for q in range(4):
            at = (q * 8 + g) * 32
            by_left_ref[q * 32 : q * 32 + 32, g * 128 : g * 128 + 128] = pair_ref[at : at + 32, :]
            by_right_ref[q * 32 : q * 32 + 32, g * 128 : g * 128 + 128] = pair32_ref[
                pl.ds(q * 8 + g, 32, stride=32), :
            ].astype(bf16)
        product = dot(by_left_ref[:, g * 128 : g * 128 + 128], head_twice, NT)
        high = product.astype(bf16).astype(f32)
        folded_ref[g * 128 : g * 128 + 128, :] = jnp.where(lane < 64, high, product - high).astype(bf16)
    row = lax.broadcasted_iota(jnp.int32, (64, 64), 0)
    col = lax.broadcasted_iota(jnp.int32, (64, 64), 1)
    own_bias = jnp.sum(jnp.where(row == col, head_bias, 0.0), axis=1, keepdims=True)
    return 2.0 * (jnp.sum(head_t.astype(f32) * pair_bias, axis=1, keepdims=True) + own_bias)


def pairs_kernel(
    place_ref, scale_ref, *refs
):
    pieces, sources, refs = refs[:8], refs[8:15], refs[15:]
    (
        loss_ref, align_grad_ref, weight_grad_ref,
        turned_ref, left_ref, plain_ref, wide_ref, flat_ref, features_ref, half_ref, dhidden_ref,
        folded_ref, by_left_ref, by_right_ref, pair32_ref,
        pair_ref, pair_bias_ref, head_ref, head_bias_ref, align_ref, gain_ref, proj_ref, sems,
    ) = refs
    transfers = fetch(sources, refs[15:22], sems)
    place = place_ref[0]
    for n, piece in enumerate(pieces):
        for k in range(4):
            sender = place ^ (n // 4 * 8 + n // 2 % 2 * 16 + n % 2 + k * 2)
            at = k * 64
            turned_ref[pl.ds(pl.multiple_of(sender * 32, 32), 32), :] = piece[at : at + 32, :].astype(f32)
            plain_ref[pl.ds(pl.multiple_of(sender * 16, 16), 16), :] = piece[at + 32 : at + 48, :]
            flat_ref[pl.ds(pl.multiple_of(sender * 16, 16), 16), :] = piece[at + 48 : at + 64, :].astype(f32)
    groups = [turned_ref[pl.ds(g, 64, stride=16), :].astype(bf16) for g in range(16)]
    for g in range(8):
        left_ref[g * 64 : g * 64 + 64, :] = groups[g]
    source = lax.broadcasted_iota(jnp.int32, (128, 512), 0)
    target = lax.broadcasted_iota(jnp.int32, (128, 512), 1)
    copies = jnp.where(source == target // 128 * 32 + target % 32, 1.0 / 32.0, 0.0).astype(bf16)
    wide_ref[...] = dot(plain_ref[...], copies).astype(bf16)

    for transfer in transfers:
        transfer.wait()
    bias = arrange_weights(
        pair_ref, pair_bias_ref[...], head_ref[...], head_bias_ref[...], folded_ref, by_left_ref, by_right_ref, pair32_ref
    )
    lane = lax.broadcasted_iota(jnp.int32, (32, 128), 1) // 32

    def forward(d, _):
        top = pl.multiple_of(d * 16, 16)
        sides = []
        for r in range(2):
            right = jnp.concatenate(
                [wide_ref[pl.ds(top, 16), (h * 2 + r) * 128 : (h * 2 + r + 1) * 128] for h in range(2)], axis=0
            )
            sides.append(
                jnp.concatenate([jnp.where(lane == q, right, jnp.zeros_like(right)) for q in range(4)], axis=0)
            )
        outer = dot(left_ref[...], jnp.concatenate(sides, axis=1)).astype(bf16)
        first = pl.multiple_of(d * 128, 128)
        features = jnp.concatenate(
            [
                jnp.concatenate([outer[g * 64 : g * 64 + 64, r * 128 : r * 128 + 128] for g in range(8)], axis=1)
                for r in range(2)
            ],
            axis=0,
        )
        features_ref[pl.ds(first, 128), :] = features
        half_ref[pl.ds(first, 128), :] = dot(features, folded_ref[...])
        return 0

    lax.fori_loop(0, 32, forward, 0, unroll=32)

    source = lax.broadcasted_iota(jnp.int32, (128, 1024), 0)
    target = lax.broadcasted_iota(jnp.int32, (128, 1024), 1)
    spread = (source == target // 64 * 8 + target % 8).astype(bf16)
    keep = (
        lax.broadcasted_iota(jnp.int32, (32, 1024), 1) // 8 % 8
        == lax.broadcasted_iota(jnp.int32, (32, 1024), 0) % 8
    )

    def blocks(row):
        placed = dot(flat_ref[pl.ds(row, 32, stride=16), :].astype(bf16), spread)
        return jnp.sum(jnp.where(keep, placed, 0.0).reshape(4, 8, 1024), axis=1)

    labels = blocks(0).astype(jnp.int32)
    mask = blocks(1)
    valid = jnp.sum(mask, keepdims=True)
    factor = mask * (scale_ref[0] / valid)
    head2 = (2.0 * head_ref[...].astype(f32).T).astype(bf16)
    bins = lax.broadcasted_iota(jnp.int32, (64, 256), 0)
    loss = jnp.zeros((1, 256), f32)
    for k in range(16):
        sums = []
        for p in range(2):
            at = k * 256 + p * 128
            j = k * 4 + p * 2
            mirrored = jnp.concatenate(
                [half_ref[pl.ds(j, 64, stride=64), :], half_ref[pl.ds(j + 1, 64, stride=64), :]], axis=0
            )
            both = (half_ref[at : at + 128, :] + mirrored).T
            sums.append(both[0:64] + both[64:128])
        logits = jnp.concatenate(sums, axis=1) + bias
        part = slice(k % 4 * 256, k % 4 * 256 + 256)
        labels_here = labels[k // 4 : k // 4 + 1, part]
        shifted = logits - jnp.max(logits, axis=0, keepdims=True)
        exp_shift = jnp.exp(shifted)
        exp_total = jnp.sum(exp_shift, axis=0, keepdims=True)
        hit = bins == labels_here
        picked = jnp.sum(jnp.where(hit, shifted, 0.0), axis=0, keepdims=True)
        loss = loss + mask[k // 4 : k // 4 + 1, part] * (jnp.log(exp_total) - picked)
        dlogits = (exp_shift / exp_total - jnp.where(hit, 1.0, 0.0)) * factor[k // 4 : k // 4 + 1, part]
        dhidden_ref[:, k * 256 : k * 256 + 256] = dot(head2, dlogits.astype(bf16)).astype(bf16)
    loss_ref[...] = jnp.sum(loss, axis=1, keepdims=True) / valid

    for n in range(4):
        turned = dot(dhidden_ref[...], features_ref[:, n * 256 : n * 256 + 256]).T
        for g in range(2):
            for q in range(4):
                at = (q * 8 + n * 2 + g) * 32
                weight_grad_ref[at : at + 32, :] = turned[g * 128 + q * 32 : g * 128 + q * 32 + 32]

    own = dhidden_ref[:, pl.ds(pl.multiple_of(place * 128, 128), 128)]
    own = jnp.concatenate([own[:, 0:64], own[:, 64:128]], axis=0)
    sums = dot(own, jnp.concatenate(groups, axis=1)).astype(bf16)

    def contract(weights, base):
        q_rows = jnp.concatenate(
            [
                jnp.concatenate(
                    [sums[r * 128 : r * 128 + 128, (base + g) * 128 : (base + g + 1) * 128] for r in range(2)], axis=1
                )
                for g in range(8)
            ],
            axis=0,
        )
        full = dot(weights, q_rows)
        row = lax.broadcasted_iota(jnp.int32, (128, 256), 0) // 32
        col = lax.broadcasted_iota(jnp.int32, (128, 256), 1) // 32 % 4
        kept = jnp.where(row == col, full, 0.0)
        return kept[0:32] + kept[32:64] + kept[64:96] + kept[96:128]

    dleft = contract(by_right_ref[...], 8)
    dright = contract(by_left_ref[...], 0)
    dproj = jnp.concatenate([dleft, dright], axis=0).T * (1.0 / 32.0)
    proj = proj_ref[...]
    proj_twice = jnp.concatenate([proj, proj], axis=0)
    align = align_ref[...].astype(f32)
    for r in range(2):
        at = r * 128
        one = dproj[at : at + 32] + dproj[at + 32 : at + 64] + dproj[at + 64 : at + 96] + dproj[at + 96 : at + 128]
        high = one.astype(bf16)
        low = (one - high.astype(f32)).astype(bf16)
        dscaled = dot(jnp.concatenate([high, low], axis=1), proj_twice) * gain_ref[...]
        scaled, inverse = layer_norm(align[:, r, :])
        align_grad_ref[:, r, :] = inverse * (
            dscaled
            - jnp.mean(dscaled, axis=-1, keepdims=True)
            - scaled * jnp.mean(dscaled * scaled, axis=-1, keepdims=True)
        )


def spec(space=pltpu.VMEM):
    return pl.BlockSpec(memory_space=space)


def far(*arrays):
    return [pltpu.with_memory_space_constraint(a, pltpu.HBM) for a in arrays]


def held(*arrays):
    return [pltpu.VMEM(a.shape, a.dtype) for a in arrays] + [pltpu.SemaphoreType.DMA((len(arrays),))]


def limit(mib):
    return pltpu.CompilerParams(vmem_limit_bytes=mib * 1024 * 1024)


def prepare(align, gain, bias, proj_t, labels_t, mask_t):
    return pl.pallas_call(
        prepare_kernel,
        out_shape=jax.ShapeDtypeStruct((64, 128), bf16),
        in_specs=[spec(pltpu.HBM)] * 6,
        out_specs=spec(),
        scratch_shapes=held(align, gain, bias, proj_t, labels_t, mask_t),
        compiler_params=limit(2),
    )(*far(align, gain, bias, proj_t, labels_t, mask_t))


def pairs(place, scale, pieces, *others):
    return pl.pallas_call(
        pairs_kernel,
        out_shape=(
            jax.ShapeDtypeStruct((1, 1), f32),
            jax.ShapeDtypeStruct((32, 2, 256), f32),
            jax.ShapeDtypeStruct((1024, 128), f32),
        ),
        in_specs=[spec(pltpu.SMEM)] * 2 + [spec()] * 8 + [spec(pltpu.HBM)] * 7,
        out_specs=(spec(),) * 3,
        scratch_shapes=[
            pltpu.VMEM((1024, 128), f32),
            pltpu.VMEM((512, 128), bf16),
            pltpu.VMEM((512, 128), bf16),
            pltpu.VMEM((512, 512), bf16),
            pltpu.VMEM((512, 128), f32),
            pltpu.VMEM((4096, 1024), bf16),
            pltpu.VMEM((4096, 128), f32),
            pltpu.VMEM((128, 4096), bf16),
            pltpu.VMEM((1024, 128), bf16),
            pltpu.VMEM((128, 1024), bf16),
            pltpu.VMEM((128, 1024), bf16),
            pltpu.VMEM((1024, 128), f32),
        ]
        + held(*others),
        compiler_params=limit(24),
    )(place, scale, *pieces, *far(*others))


def join_kernel(*refs):
    for n, part in enumerate(refs[:4]):
        refs[4][n * 64 : n * 64 + 64, :] = part[...]


def join(parts):
    return pl.pallas_call(
        join_kernel,
        out_shape=jax.ShapeDtypeStruct((256, 128), bf16),
        in_specs=[spec()] * 4,
        out_specs=spec(),
        compiler_params=limit(2),
    )(*parts)


def gather(message):
    def swap(block, row_bits, col_bits):
        moves = [(d, (d // 8 ^ row_bits) * 8 + (d % 8 ^ col_bits)) for d in range(32)]
        return lax.ppermute(block, ("row", "col"), moves)

    line = join([message] + [swap(message, 0, 2 * k) for k in range(1, 4)])
    plane = [line] + [swap(line, n // 2 * 2, n % 2) for n in range(1, 4)]
    return plane + [swap(block, 1, 0) for block in plane]


def local_whole(
    alignment, norm_gain, norm_bias, proj_weight, pair_weight, pair_bias, head_weight, head_bias,
    labels, pair_mask, loss_scale,
):
    gain = norm_gain.reshape(1, 256)
    message = prepare(alignment, gain, norm_bias.reshape(1, 256), proj_weight.T, labels.T, pair_mask.T)
    pieces = gather(message)
    place = lax.axis_index(("row", "col")).astype(jnp.int32).reshape(1)
    loss, align_grad, weight_grad = pairs(
        place, loss_scale.reshape(1), pieces, pair_weight, pair_bias.reshape(1, 128), head_weight.T,
        head_bias.reshape(1, 64), alignment, gain, proj_weight.T,
    )
    return (loss.reshape(()), align_grad, weight_grad)


def solution(mesh):
    in_specs = (
        P(None, ("row", "col"), None),
        P(),
        P(),
        P(),
        P(),
        P(),
        P(),
        P(),
        P("row", "col"),
        P("row", "col"),
        P(),
    )
    out_specs = (P(), P(None, ("row", "col"), None), P())
    def whole(alignment, *others):
        sequences, residues, channels = alignment.shape
        small = (
            (sequences, residues, channels) == (32, 64, 256)
            and tuple(mesh.shape.values()) == (4, 8)
            and others[2].shape[1] == 64
            and others[3].shape == (1024, 128)
            and others[5].shape == (128, 64)
        )
        return jax.shard_map(
            local_whole if small else local, mesh=mesh, in_specs=in_specs, out_specs=out_specs, check_vma=False
        )(alignment, *others)

    return whole
```

```python
import functools

import jax
import jax.numpy as jnp
from jax import lax
from jax.experimental import pallas as pl
from jax.experimental.pallas import tpu as pltpu
from jax.sharding import PartitionSpec as P

norm_eps = 1e-05
highest = lax.Precision.HIGHEST


def from_root(value, axis, source):
    kept = jnp.where(lax.axis_index(axis) == source, value, 0).astype(value.dtype)
    return lax.psum(kept, axis)


def normalize(alignment, norm_gain, norm_bias):
    values = alignment.astype(jnp.float32)
    centered = values - jnp.mean(values, axis=-1, keepdims=True)
    inverse = lax.rsqrt(jnp.mean(centered * centered, axis=-1, keepdims=True) + norm_eps)
    scaled = centered * inverse
    normed = (scaled * norm_gain + norm_bias).astype(jnp.bfloat16)
    return (scaled, inverse, normed)


def pair_features(left_proj, right_proj, mirrored):
    if mirrored:
        outer = jnp.einsum(
            "sid,sjc->ijcd", left_proj, right_proj, preferred_element_type=jnp.float32
        )
    else:
        outer = jnp.einsum(
            "sic,sjd->ijcd", left_proj, right_proj, preferred_element_type=jnp.float32
        )
    outer = outer * (1.0 / left_proj.shape[0])
    return outer.astype(jnp.bfloat16).reshape(-1, outer.shape[2] * outer.shape[3])


def local(
    alignment,
    norm_gain,
    norm_bias,
    proj_weight,
    pair_weight,
    pair_bias,
    head_weight,
    head_bias,
    labels,
    pair_mask,
    loss_scale,
):
    per_row = lax.axis_size("col") // lax.axis_size("row")
    col_place = lax.axis_index("col")
    row_place = lax.axis_index("row")
    sequences = alignment.shape[0]
    outer_width = proj_weight.shape[1] // 2
    bin_count = head_weight.shape[1]
    scaled, inverse, normed = normalize(alignment, norm_gain, norm_bias)
    projected = jnp.einsum(
        "src,cp->srp", normed, proj_weight, preferred_element_type=jnp.float32
    ).astype(jnp.bfloat16)
    mask_values = pair_mask.astype(jnp.float32)
    valid_pairs = lax.psum(jnp.sum(mask_values), ("row", "col"))
    row_proj = lax.all_gather(projected, "col", axis=1, tiled=True)
    row_span = row_proj.shape[1]
    col_span = row_span // per_row
    offset = col_place % per_row * col_span
    own_slice = lax.dynamic_slice_in_dim(row_proj, offset, col_span, 1)
    col_proj = from_root(own_slice, "row", col_place // per_row)
    pair32 = pair_weight.astype(jnp.float32)
    head32 = head_weight.astype(jnp.float32)
    weight_shape = pair32.shape
    grad_width = 2 * outer_width
    block_rows = min(row_span, max(1, 512 // col_span))
    num_blocks = row_span // block_rows
    grad_factor = loss_scale / valid_pairs
    inv_seqs = 1.0 / sequences
    bins_iota = lax.broadcasted_iota(jnp.int32, (block_rows * col_span, bin_count), 1)

    def pair_head(features):
        hidden = jnp.dot(features, pair_weight, preferred_element_type=jnp.float32) + pair_bias
        return jnp.dot(hidden, head32, precision=highest) + head_bias

    def tile_back(features, dhalf, left_proj, right_proj, mirrored):
        dhidden = jnp.dot(dhalf, head_weight.T, preferred_element_type=jnp.float32)
        dfeatures = jnp.dot(dhidden, pair32.T, precision=highest)
        weight_term = jnp.dot(features.astype(jnp.float32).T, dhidden, precision=highest)
        dfeatures = dfeatures.astype(jnp.bfloat16).reshape(
            left_proj.shape[1], right_proj.shape[1], outer_width, outer_width
        )
        if mirrored:
            grad_left = jnp.einsum(
                "ijcd,sjc->sid", dfeatures, right_proj, preferred_element_type=jnp.float32
            )
            grad_right = jnp.einsum(
                "ijcd,sid->sjc", dfeatures, left_proj, preferred_element_type=jnp.float32
            )
        else:
            grad_left = jnp.einsum(
                "ijcd,sjd->sic", dfeatures, right_proj, preferred_element_type=jnp.float32
            )
            grad_right = jnp.einsum(
                "ijcd,sic->sjd", dfeatures, left_proj, preferred_element_type=jnp.float32
            )
        return (grad_left * inv_seqs, grad_right * inv_seqs, weight_term)

    def block_step(block_index, carry):
        loss_sum, weight_sum, row_grad, col_grad = carry
        first_row = block_index * block_rows
        rows_here = lax.dynamic_slice_in_dim(row_proj, first_row, block_rows, 1)
        left_own = rows_here[:, :, :outer_width]
        left_mirror = rows_here[:, :, outer_width:]
        right_own = col_proj[:, :, outer_width:]
        right_mirror = col_proj[:, :, :outer_width]
        own_features = pair_features(left_own, right_own, False)
        mirror_features = pair_features(left_mirror, right_mirror, True)
        logits = pair_head(own_features) + pair_head(mirror_features)
        labels_here = lax.dynamic_slice_in_dim(labels, first_row, block_rows, 0).reshape(-1)
        mask_here = lax.dynamic_slice_in_dim(mask_values, first_row, block_rows, 0).reshape(-1)
        row_top = jnp.max(logits, axis=-1, keepdims=True)
        shifted = logits - row_top
        exp_shift = jnp.exp(shifted)
        exp_total = jnp.sum(exp_shift, axis=-1, keepdims=True)
        target = bins_iota == labels_here[:, None]
        picked = jnp.sum(jnp.where(target, shifted, 0.0), axis=-1)
        loss_sum = loss_sum + jnp.sum(mask_here * (jnp.log(exp_total[:, 0]) - picked))
        dlogits = (
            (exp_shift / exp_total - target.astype(jnp.float32))
            * (mask_here * grad_factor)[:, None]
        ).astype(jnp.bfloat16)
        grad_left, grad_right, weight_term = tile_back(
            own_features, dlogits, left_own, right_own, False
        )
        mirror_left, mirror_right, mirror_term = tile_back(
            mirror_features, dlogits, left_mirror, right_mirror, True
        )
        row_part = jnp.concatenate([grad_left, mirror_left], axis=-1)
        col_part = jnp.concatenate([mirror_right, grad_right], axis=-1)
        weight_term = weight_term + mirror_term
        row_grad = lax.dynamic_update_slice_in_dim(row_grad, row_part, first_row, 1)
        return (loss_sum, weight_sum + weight_term, row_grad, col_grad + col_part)

    initial = (
        jnp.zeros((), jnp.float32),
        jnp.zeros(weight_shape, jnp.float32),
        jnp.zeros((sequences, row_span, grad_width), jnp.float32),
        jnp.zeros((sequences, col_span, grad_width), jnp.float32),
    )
    loss_sum, weight_sum, row_grad, col_grad = lax.fori_loop(0, num_blocks, block_step, initial)
    holder = col_place // per_row == row_place
    col_sum = lax.psum(col_grad.astype(jnp.bfloat16), "row").astype(jnp.float32)
    placed = lax.dynamic_update_slice_in_dim(jnp.zeros_like(row_grad), col_sum, offset, 1)
    contribution = row_grad + jnp.where(holder, placed, 0.0)
    own_grad = lax.psum_scatter(contribution, "col", scatter_dimension=1, tiled=True)
    dnormed = jnp.einsum(
        "srp,cp->src", own_grad, proj_weight.astype(jnp.float32), precision=highest
    )
    dscaled = dnormed * norm_gain
    alignment_grad = inverse * (
        dscaled
        - jnp.mean(dscaled, axis=-1, keepdims=True)
        - scaled * jnp.mean(dscaled * scaled, axis=-1, keepdims=True)
    )
    loss_total, pair_weight_grad = lax.psum((loss_sum, weight_sum), ("row", "col"))
    return (loss_total / valid_pairs, alignment_grad, pair_weight_grad)


f32 = jnp.float32
bf16 = jnp.bfloat16
NN = (((1,), (0,)), ((), ()))
NT = (((1,), (1,)), ((), ()))


def dot(a, b, dims=NN):
    return lax.dot_general(a, b, dims, preferred_element_type=f32)


def layer_norm(x):
    centered = x - jnp.mean(x, axis=-1, keepdims=True)
    inverse = lax.rsqrt(jnp.mean(centered * centered, axis=-1, keepdims=True) + norm_eps)
    return centered * inverse, inverse


def fetch(sources, targets, sems):
    copies = [
        pltpu.make_async_copy(source, target, sems.at[n])
        for n, (source, target) in enumerate(zip(sources, targets, strict=True))
    ]
    for copy in copies:
        copy.start()
    return copies


def prepare_kernel(*refs):
    sources, out_ref, near, scratch, sems = refs[:10], refs[10], refs[11:18], refs[18:21], refs[21]
    align_ref, gain_ref, weight_ref = near[:3]
    bias_ref, labels_ref, mask_ref = scratch
    copies = fetch(sources, near[:3] + scratch + near[3:], sems)
    for copy in copies[:6]:
        copy.wait()
    align = align_ref[...].astype(f32)
    weight = weight_ref[...]
    plain = []
    for r in range(2):
        scaled, _ = layer_norm(align[:, r, :])
        normed = (scaled * gain_ref[...] + bias_ref[...]).astype(bf16)
        turned = dot(weight, normed, NT)
        rows = [
            jnp.concatenate([turned[h * 32 + q * 8 : h * 32 + q * 8 + 8] for q in range(4)], axis=1)
            for h in range(2)
        ]
        out_ref[r * 16 : r * 16 + 16, :] = jnp.concatenate(rows, axis=0).astype(bf16)
        plain.append(dot(normed, weight[32:64], NT))
    out_ref[32:48, :] = jnp.concatenate(
        [plain[r][h * 16 : h * 16 + 16] for h in range(2) for r in range(2)], axis=1
    ).astype(bf16)
    lane = lax.broadcasted_iota(jnp.int32, (16, 128), 1)
    spread = (lane // 8 == lax.broadcasted_iota(jnp.int32, (16, 128), 0)).astype(bf16)
    keep = lane[:8] % 8 == lax.broadcasted_iota(jnp.int32, (8, 128), 0)
    flat = []
    for ref in (labels_ref, mask_ref):
        wide = dot(ref[...].astype(f32).astype(bf16), spread)
        flat.append(jnp.sum(jnp.where(keep, wide, 0.0), axis=0, keepdims=True))
    row = lax.broadcasted_iota(jnp.int32, (16, 128), 0)
    out_ref[48:64, :] = jnp.where(row == 0, flat[0], jnp.where(row == 1, flat[1], 0.0)).astype(bf16)
    for copy in copies[6:]:
        copy.wait()


def weights_kernel(
    pair_ref, pair_bias_ref, head_ref, head_bias_ref, folded_ref, by_left_ref, by_right_ref, bias_ref, pair32_ref
):
    head_t = head_ref[...]
    pair32_ref[...] = pair_ref[...].astype(f32)
    head_twice = jnp.concatenate([head_t, head_t], axis=0)
    lane = lax.broadcasted_iota(jnp.int32, (128, 128), 1)
    for g in range(8):
        for q in range(4):
            at = (q * 8 + g) * 32
            by_left_ref[q * 32 : q * 32 + 32, g * 128 : g * 128 + 128] = pair_ref[at : at + 32, :]
            by_right_ref[q * 32 : q * 32 + 32, g * 128 : g * 128 + 128] = pair32_ref[
                pl.ds(q * 8 + g, 32, stride=32), :
            ].astype(bf16)
        product = dot(by_left_ref[:, g * 128 : g * 128 + 128], head_twice, NT)
        high = product.astype(bf16).astype(f32)
        folded_ref[g * 128 : g * 128 + 128, :] = jnp.where(lane < 64, high, product - high).astype(bf16)
    row = lax.broadcasted_iota(jnp.int32, (64, 64), 0)
    col = lax.broadcasted_iota(jnp.int32, (64, 64), 1)
    own_bias = jnp.sum(jnp.where(row == col, head_bias_ref[...], 0.0), axis=1, keepdims=True)
    bias_ref[...] = 2.0 * (jnp.sum(head_t.astype(f32) * pair_bias_ref[...], axis=1, keepdims=True) + own_bias)


def pairs_kernel(
    place_ref, scale_ref, *refs
):
    pieces, refs = refs[:8], refs[8:]
    (
        folded_ref, by_left_ref, by_right_ref, bias_ref, head_ref, align_ref, gain_ref, proj_ref,
        loss_ref, align_grad_ref, weight_grad_ref,
        turned_ref, left_ref, plain_ref, wide_ref, flat_ref, features_ref, half_ref, dhidden_ref,
    ) = refs
    place = place_ref[0]
    for n, piece in enumerate(pieces):
        for k in range(4):
            sender = place ^ (n // 4 * 8 + n // 2 % 2 * 16 + n % 2 + k * 2)
            at = k * 64
            turned_ref[pl.ds(pl.multiple_of(sender * 32, 32), 32), :] = piece[at : at + 32, :].astype(f32)
            plain_ref[pl.ds(pl.multiple_of(sender * 16, 16), 16), :] = piece[at + 32 : at + 48, :]
            flat_ref[pl.ds(pl.multiple_of(sender * 16, 16), 16), :] = piece[at + 48 : at + 64, :].astype(f32)
    groups = [
        jnp.concatenate([turned_ref[pl.ds(p * 16 + g, 32, stride=32), :] for p in range(2)], axis=0).astype(bf16)
        for g in range(16)
    ]
    for g in range(8):
        left_ref[g * 64 : g * 64 + 64, :] = groups[g]
    source = lax.broadcasted_iota(jnp.int32, (128, 512), 0)
    target = lax.broadcasted_iota(jnp.int32, (128, 512), 1)
    copies = jnp.where(source == target // 128 * 32 + target % 32, 1.0 / 32.0, 0.0).astype(bf16)
    wide_ref[...] = dot(plain_ref[...], copies).astype(bf16)

    lane = lax.broadcasted_iota(jnp.int32, (32, 128), 1) // 32

    def outer_products(d):
        sides = []
        for r in range(2):
            right = jnp.concatenate(
                [wide_ref[d * 16 : d * 16 + 16, (h * 2 + r) * 128 : (h * 2 + r + 1) * 128] for h in range(2)], axis=0
            )
            sides.append(
                jnp.concatenate([jnp.where(lane == q, right, jnp.zeros_like(right)) for q in range(4)], axis=0)
            )
        outer = dot(left_ref[...], jnp.concatenate(sides, axis=1)).astype(bf16)
        for r in range(2):
            for p in range(2):
                at = d // 2 * 256 + (p + r) % 2 * 128 + d % 2 * 64 + r * 32
                for g in range(8):
                    features_ref[at : at + 32, g * 128 : g * 128 + 128] = outer[
                        g * 64 + p * 32 : g * 64 + p * 32 + 32, r * 128 : r * 128 + 128
                    ]

    side = lax.broadcasted_iota(jnp.int32, (128, 128), 1) < 64

    def half_logits(d):
        at = d // 2 * 256 + d % 2 * 64
        rows = jnp.concatenate([features_ref[at + h : at + h + 64, :] for h in (0, 128)], axis=0)
        part = dot(rows, folded_ref[...])
        part = part + pltpu.roll(part, 64, 1)
        half_ref[d * 64 : d * 64 + 64, :] = jnp.where(side[0:64], part[0:64], part[64:128])

    early = 2
    for d in range(early):
        outer_products(d)
    for d in range(32):
        if d + early < 32:
            outer_products(d + early)
        half_logits(d)

    source = lax.broadcasted_iota(jnp.int32, (128, 1024), 0)
    target = lax.broadcasted_iota(jnp.int32, (128, 1024), 1)
    first = target // 256 * 4 + target // 32 % 4
    second = target % 32 * 2 + (target // 128 + first) % 2
    spread = (source == first * 8 + second % 8).astype(bf16)
    keep = second[0:32] // 8 == lax.broadcasted_iota(jnp.int32, (32, 1024), 0) % 8

    def blocks(row):
        placed = dot(flat_ref[pl.ds(row, 32, stride=16), :].astype(bf16), spread)
        return jnp.sum(jnp.where(keep, placed, 0.0).reshape(4, 8, 1024), axis=1)

    labels = blocks(0).astype(jnp.int32)
    mask = blocks(1)
    valid = jnp.sum(mask, keepdims=True)
    factor = mask * (scale_ref[0] / valid)
    head2 = (2.0 * head_ref[...].astype(f32).T).astype(bf16)
    bins = lax.broadcasted_iota(jnp.int32, (64, 256), 0)
    loss = jnp.zeros((1, 256), f32)
    for k in range(16):
        rows = []
        for j in (k * 2, k * 2 + 1):
            even = half_ref[pl.ds(j, 32, stride=64), :]
            odd = half_ref[pl.ds(j + 32, 32, stride=64), :]
            rows += [jnp.where(side[0:32], even, odd), jnp.where(side[0:32], odd, even)]
        both = (half_ref[k * 128 : k * 128 + 128, :] + jnp.concatenate(rows, axis=0)).T
        logits = jnp.concatenate([both[0:64], both[64:128]], axis=1) + bias_ref[...]
        part = slice(k % 4 * 256, k % 4 * 256 + 256)
        labels_here = labels[k // 4 : k // 4 + 1, part]
        shifted = logits - jnp.max(logits, axis=0, keepdims=True)
        exp_shift = jnp.exp(shifted)
        exp_total = jnp.sum(exp_shift, axis=0, keepdims=True)
        hit = bins == labels_here
        picked = jnp.sum(jnp.where(hit, shifted, 0.0), axis=0, keepdims=True)
        loss = loss + mask[k // 4 : k // 4 + 1, part] * (jnp.log(exp_total) - picked)
        here = factor[k // 4 : k // 4 + 1, part]
        dlogits = exp_shift * (here / exp_total) - jnp.where(hit, here, 0.0)
        dhidden_ref[:, k * 256 : k * 256 + 256] = dot(head2, dlogits.astype(bf16)).astype(bf16)
    loss_ref[...] = jnp.sum(loss, axis=1, keepdims=True) / valid

    for n in range(4):
        turned = dot(dhidden_ref[...], features_ref[:, n * 256 : n * 256 + 256]).T
        for g in range(2):
            for q in range(4):
                at = (q * 8 + n * 2 + g) * 32
                weight_grad_ref[at : at + 32, :] = turned[g * 128 + q * 32 : g * 128 + q * 32 + 32]

    own = dhidden_ref[:, pl.ds(pl.multiple_of(place // 2 * 256, 256), 256)]
    own = [jnp.where(place % 2 == 0, own[:, n : n + 64], own[:, n + 64 : n + 128]) for n in (0, 128)]
    own = jnp.concatenate(
        [
            jnp.concatenate([own[0][:, 0:32], own[1][:, 0:32]], axis=1),
            jnp.concatenate([own[1][:, 32:64], own[0][:, 32:64]], axis=1),
        ],
        axis=0,
    )
    sums = dot(own, jnp.concatenate(groups, axis=1)).astype(bf16)

    def contract(weights, base):
        q_rows = jnp.concatenate(
            [
                jnp.concatenate(
                    [sums[r * 128 : r * 128 + 128, (base + g) * 128 : (base + g + 1) * 128] for r in range(2)], axis=1
                )
                for g in range(8)
            ],
            axis=0,
        )
        full = dot(weights, q_rows)
        row = lax.broadcasted_iota(jnp.int32, (128, 256), 0) // 32
        col = lax.broadcasted_iota(jnp.int32, (128, 256), 1) // 32 % 4
        kept = jnp.where(row == col, full, 0.0)
        return kept[0:32] + kept[32:64] + kept[64:96] + kept[96:128]

    dleft = contract(by_right_ref[...], 8)
    dright = contract(by_left_ref[...], 0)
    dproj = jnp.concatenate([dleft, dright], axis=0).T * (1.0 / 32.0)
    proj = proj_ref[...]
    proj_twice = jnp.concatenate([proj, proj], axis=0)
    align = align_ref[...].astype(f32)
    for r in range(2):
        at = r * 128
        one = dproj[at : at + 32] + dproj[at + 32 : at + 64] + dproj[at + 64 : at + 96] + dproj[at + 96 : at + 128]
        high = one.astype(bf16)
        low = (one - high.astype(f32)).astype(bf16)
        dscaled = dot(jnp.concatenate([high, low], axis=1), proj_twice) * gain_ref[...]
        scaled, inverse = layer_norm(align[:, r, :])
        align_grad_ref[:, r, :] = inverse * (
            dscaled
            - jnp.mean(dscaled, axis=-1, keepdims=True)
            - scaled * jnp.mean(dscaled * scaled, axis=-1, keepdims=True)
        )


def spec(space=pltpu.VMEM):
    return pl.BlockSpec(memory_space=space)


def far(*arrays):
    return [pltpu.with_memory_space_constraint(a, pltpu.HBM) for a in arrays]


def held(*arrays):
    return [pltpu.VMEM(a.shape, a.dtype) for a in arrays]


def limit(mib):
    return pltpu.CompilerParams(vmem_limit_bytes=mib * 1024 * 1024)


def prepare(align, gain, proj_t, bias, labels_t, mask_t, *others):
    near = (align, gain, proj_t) + others
    local = (bias, labels_t, mask_t)
    return pl.pallas_call(
        prepare_kernel,
        out_shape=[jax.ShapeDtypeStruct((64, 128), bf16)] + [jax.ShapeDtypeStruct(a.shape, a.dtype) for a in near],
        in_specs=[spec(pltpu.HBM)] * 10,
        out_specs=[spec()] * 8,
        scratch_shapes=held(*local) + [pltpu.SemaphoreType.DMA((10,))],
        compiler_params=limit(2),
    )(*far(*near[:3], *local, *others))


def weights(*operands):
    return pl.pallas_call(
        weights_kernel,
        out_shape=(
            jax.ShapeDtypeStruct((1024, 128), bf16),
            jax.ShapeDtypeStruct((128, 1024), bf16),
            jax.ShapeDtypeStruct((128, 1024), bf16),
            jax.ShapeDtypeStruct((64, 1), f32),
        ),
        in_specs=[spec()] * 4,
        out_specs=[spec()] * 4,
        scratch_shapes=[pltpu.VMEM((1024, 128), f32)],
        compiler_params=limit(4),
    )(*operands)


def pairs(place, scale, pieces, *others):
    return pl.pallas_call(
        pairs_kernel,
        out_shape=(
            jax.ShapeDtypeStruct((1, 1), f32),
            jax.ShapeDtypeStruct((32, 2, 256), f32),
            jax.ShapeDtypeStruct((1024, 128), f32),
        ),
        in_specs=[spec(pltpu.SMEM)] * 2 + [spec()] * 16,
        out_specs=(spec(),) * 3,
        scratch_shapes=[
            pltpu.VMEM((1024, 128), f32),
            pltpu.VMEM((512, 128), bf16),
            pltpu.VMEM((512, 128), bf16),
            pltpu.VMEM((512, 512), bf16),
            pltpu.VMEM((512, 128), f32),
            pltpu.VMEM((4096, 1024), bf16),
            pltpu.VMEM((2048, 128), f32),
            pltpu.VMEM((128, 4096), bf16),
        ],
        compiler_params=limit(24),
    )(place, scale, *pieces, *others)


def join_kernel(*refs):
    for n, part in enumerate(refs[:4]):
        refs[4][n * 64 : n * 64 + 64, :] = part[...]


def join(parts):
    return pl.pallas_call(
        join_kernel,
        out_shape=jax.ShapeDtypeStruct((256, 128), bf16),
        in_specs=[spec()] * 4,
        out_specs=spec(),
        compiler_params=limit(2),
    )(*parts)


def gather(message):
    def swap(block, row_bits, col_bits):
        moves = [(d, (d // 8 ^ row_bits) * 8 + (d % 8 ^ col_bits)) for d in range(32)]
        return lax.ppermute(block, ("row", "col"), moves)

    line = join([message] + [swap(message, 0, 2 * k) for k in range(1, 4)])
    plane = [line] + [swap(line, n // 2 * 2, n % 2) for n in range(1, 4)]
    return plane + [swap(block, 1, 0) for block in plane]


def local_whole(
    alignment, norm_gain, norm_bias, proj_weight, pair_weight, pair_bias, head_weight, head_bias,
    labels, pair_mask, loss_scale,
):
    message, align, gain, proj_t, pair, pair_bias, head_t, head_bias = prepare(
        alignment, norm_gain.reshape(1, 256), proj_weight.T, norm_bias.reshape(1, 256), labels.T, pair_mask.T,
        pair_weight, pair_bias.reshape(1, 128), head_weight.T, head_bias.reshape(1, 64),
    )
    arranged = weights(pair, pair_bias, head_t, head_bias)
    pieces = gather(message)
    place = lax.axis_index(("row", "col")).astype(jnp.int32).reshape(1)
    loss, align_grad, weight_grad = pairs(
        place, loss_scale.reshape(1), pieces, *arranged, head_t, align, gain, proj_t
    )
    return (loss.reshape(()), align_grad, weight_grad)


def solution(mesh):
    in_specs = (
        P(None, ("row", "col"), None),
        P(),
        P(),
        P(),
        P(),
        P(),
        P(),
        P(),
        P("row", "col"),
        P("row", "col"),
        P(),
    )
    out_specs = (P(), P(None, ("row", "col"), None), P())
    def whole(alignment, *others):
        sequences, residues, channels = alignment.shape
        small = (
            (sequences, residues, channels) == (32, 64, 256)
            and tuple(mesh.shape.values()) == (4, 8)
            and others[2].shape[1] == 64
            and others[3].shape == (1024, 128)
            and others[5].shape == (128, 64)
        )
        return jax.shard_map(
            local_whole if small else local, mesh=mesh, in_specs=in_specs, out_specs=out_specs, check_vma=False
        )(alignment, *others)

    return whole
```

```python
import functools

import jax
import jax.numpy as jnp
from jax import lax
from jax.experimental import pallas as pl
from jax.experimental.pallas import tpu as pltpu
from jax.sharding import PartitionSpec as P

norm_eps = 1e-05
highest = lax.Precision.HIGHEST


def from_root(value, axis, source):
    kept = jnp.where(lax.axis_index(axis) == source, value, 0).astype(value.dtype)
    return lax.psum(kept, axis)


def normalize(alignment, norm_gain, norm_bias):
    values = alignment.astype(jnp.float32)
    centered = values - jnp.mean(values, axis=-1, keepdims=True)
    inverse = lax.rsqrt(jnp.mean(centered * centered, axis=-1, keepdims=True) + norm_eps)
    scaled = centered * inverse
    normed = (scaled * norm_gain + norm_bias).astype(jnp.bfloat16)
    return (scaled, inverse, normed)


def pair_features(left_proj, right_proj, mirrored):
    if mirrored:
        outer = jnp.einsum(
            "sid,sjc->ijcd", left_proj, right_proj, preferred_element_type=jnp.float32
        )
    else:
        outer = jnp.einsum(
            "sic,sjd->ijcd", left_proj, right_proj, preferred_element_type=jnp.float32
        )
    outer = outer * (1.0 / left_proj.shape[0])
    return outer.astype(jnp.bfloat16).reshape(-1, outer.shape[2] * outer.shape[3])


def local(
    alignment,
    norm_gain,
    norm_bias,
    proj_weight,
    pair_weight,
    pair_bias,
    head_weight,
    head_bias,
    labels,
    pair_mask,
    loss_scale,
):
    per_row = lax.axis_size("col") // lax.axis_size("row")
    col_place = lax.axis_index("col")
    row_place = lax.axis_index("row")
    sequences = alignment.shape[0]
    outer_width = proj_weight.shape[1] // 2
    bin_count = head_weight.shape[1]
    scaled, inverse, normed = normalize(alignment, norm_gain, norm_bias)
    projected = jnp.einsum(
        "src,cp->srp", normed, proj_weight, preferred_element_type=jnp.float32
    ).astype(jnp.bfloat16)
    mask_values = pair_mask.astype(jnp.float32)
    valid_pairs = lax.psum(jnp.sum(mask_values), ("row", "col"))
    row_proj = lax.all_gather(projected, "col", axis=1, tiled=True)
    row_span = row_proj.shape[1]
    col_span = row_span // per_row
    offset = col_place % per_row * col_span
    own_slice = lax.dynamic_slice_in_dim(row_proj, offset, col_span, 1)
    col_proj = from_root(own_slice, "row", col_place // per_row)
    pair32 = pair_weight.astype(jnp.float32)
    head32 = head_weight.astype(jnp.float32)
    weight_shape = pair32.shape
    grad_width = 2 * outer_width
    block_rows = min(row_span, max(1, 512 // col_span))
    num_blocks = row_span // block_rows
    grad_factor = loss_scale / valid_pairs
    inv_seqs = 1.0 / sequences
    bins_iota = lax.broadcasted_iota(jnp.int32, (block_rows * col_span, bin_count), 1)

    def pair_head(features):
        hidden = jnp.dot(features, pair_weight, preferred_element_type=jnp.float32) + pair_bias
        return jnp.dot(hidden, head32, precision=highest) + head_bias

    def tile_back(features, dhalf, left_proj, right_proj, mirrored):
        dhidden = jnp.dot(dhalf, head_weight.T, preferred_element_type=jnp.float32)
        dfeatures = jnp.dot(dhidden, pair32.T, precision=highest)
        weight_term = jnp.dot(features.astype(jnp.float32).T, dhidden, precision=highest)
        dfeatures = dfeatures.astype(jnp.bfloat16).reshape(
            left_proj.shape[1], right_proj.shape[1], outer_width, outer_width
        )
        if mirrored:
            grad_left = jnp.einsum(
                "ijcd,sjc->sid", dfeatures, right_proj, preferred_element_type=jnp.float32
            )
            grad_right = jnp.einsum(
                "ijcd,sid->sjc", dfeatures, left_proj, preferred_element_type=jnp.float32
            )
        else:
            grad_left = jnp.einsum(
                "ijcd,sjd->sic", dfeatures, right_proj, preferred_element_type=jnp.float32
            )
            grad_right = jnp.einsum(
                "ijcd,sic->sjd", dfeatures, left_proj, preferred_element_type=jnp.float32
            )
        return (grad_left * inv_seqs, grad_right * inv_seqs, weight_term)

    def block_step(block_index, carry):
        loss_sum, weight_sum, row_grad, col_grad = carry
        first_row = block_index * block_rows
        rows_here = lax.dynamic_slice_in_dim(row_proj, first_row, block_rows, 1)
        left_own = rows_here[:, :, :outer_width]
        left_mirror = rows_here[:, :, outer_width:]
        right_own = col_proj[:, :, outer_width:]
        right_mirror = col_proj[:, :, :outer_width]
        own_features = pair_features(left_own, right_own, False)
        mirror_features = pair_features(left_mirror, right_mirror, True)
        logits = pair_head(own_features) + pair_head(mirror_features)
        labels_here = lax.dynamic_slice_in_dim(labels, first_row, block_rows, 0).reshape(-1)
        mask_here = lax.dynamic_slice_in_dim(mask_values, first_row, block_rows, 0).reshape(-1)
        row_top = jnp.max(logits, axis=-1, keepdims=True)
        shifted = logits - row_top
        exp_shift = jnp.exp(shifted)
        exp_total = jnp.sum(exp_shift, axis=-1, keepdims=True)
        target = bins_iota == labels_here[:, None]
        picked = jnp.sum(jnp.where(target, shifted, 0.0), axis=-1)
        loss_sum = loss_sum + jnp.sum(mask_here * (jnp.log(exp_total[:, 0]) - picked))
        dlogits = (
            (exp_shift / exp_total - target.astype(jnp.float32))
            * (mask_here * grad_factor)[:, None]
        ).astype(jnp.bfloat16)
        grad_left, grad_right, weight_term = tile_back(
            own_features, dlogits, left_own, right_own, False
        )
        mirror_left, mirror_right, mirror_term = tile_back(
            mirror_features, dlogits, left_mirror, right_mirror, True
        )
        row_part = jnp.concatenate([grad_left, mirror_left], axis=-1)
        col_part = jnp.concatenate([mirror_right, grad_right], axis=-1)
        weight_term = weight_term + mirror_term
        row_grad = lax.dynamic_update_slice_in_dim(row_grad, row_part, first_row, 1)
        return (loss_sum, weight_sum + weight_term, row_grad, col_grad + col_part)

    initial = (
        jnp.zeros((), jnp.float32),
        jnp.zeros(weight_shape, jnp.float32),
        jnp.zeros((sequences, row_span, grad_width), jnp.float32),
        jnp.zeros((sequences, col_span, grad_width), jnp.float32),
    )
    loss_sum, weight_sum, row_grad, col_grad = lax.fori_loop(0, num_blocks, block_step, initial)
    holder = col_place // per_row == row_place
    col_sum = lax.psum(col_grad.astype(jnp.bfloat16), "row").astype(jnp.float32)
    placed = lax.dynamic_update_slice_in_dim(jnp.zeros_like(row_grad), col_sum, offset, 1)
    contribution = row_grad + jnp.where(holder, placed, 0.0)
    own_grad = lax.psum_scatter(contribution, "col", scatter_dimension=1, tiled=True)
    dnormed = jnp.einsum(
        "srp,cp->src", own_grad, proj_weight.astype(jnp.float32), precision=highest
    )
    dscaled = dnormed * norm_gain
    alignment_grad = inverse * (
        dscaled
        - jnp.mean(dscaled, axis=-1, keepdims=True)
        - scaled * jnp.mean(dscaled * scaled, axis=-1, keepdims=True)
    )
    loss_total, pair_weight_grad = lax.psum((loss_sum, weight_sum), ("row", "col"))
    return (loss_total / valid_pairs, alignment_grad, pair_weight_grad)


f32 = jnp.float32
bf16 = jnp.bfloat16
NN = (((1,), (0,)), ((), ()))
NT = (((1,), (1,)), ((), ()))


def dot(a, b, dims=NN):
    return lax.dot_general(a, b, dims, preferred_element_type=f32)


def layer_norm(x):
    centered = x - jnp.mean(x, axis=-1, keepdims=True)
    inverse = lax.rsqrt(jnp.mean(centered * centered, axis=-1, keepdims=True) + norm_eps)
    return centered * inverse, inverse


def fetch(sources, targets, sems):
    copies = [
        pltpu.make_async_copy(source, target, sems.at[n])
        for n, (source, target) in enumerate(zip(sources, targets, strict=True))
    ]
    for copy in copies:
        copy.start()
    return copies


def prepare_kernel(*refs):
    sources, out_ref, near, scratch, sems = refs[:10], refs[10], refs[11:18], refs[18:21], refs[21]
    align_ref, gain_ref, weight_ref = near[:3]
    bias_ref, labels_ref, mask_ref = scratch
    copies = fetch(sources, near[:3] + scratch + near[3:], sems)
    for copy in copies[:6]:
        copy.wait()
    align = align_ref[...].astype(f32)
    weight = weight_ref[...]
    plain = []
    for r in range(2):
        scaled, _ = layer_norm(align[:, r, :])
        normed = (scaled * gain_ref[...] + bias_ref[...]).astype(bf16)
        turned = dot(weight, normed, NT)
        rows = [
            jnp.concatenate([turned[h * 32 + q * 8 : h * 32 + q * 8 + 8] for q in range(4)], axis=1)
            for h in range(2)
        ]
        out_ref[r * 16 : r * 16 + 16, :] = jnp.concatenate(rows, axis=0).astype(bf16)
        plain.append(dot(normed, weight[32:64], NT))
    out_ref[32:48, :] = jnp.concatenate(
        [plain[r][h * 16 : h * 16 + 16] for h in range(2) for r in range(2)], axis=1
    ).astype(bf16)
    lane = lax.broadcasted_iota(jnp.int32, (16, 128), 1)
    spread = (lane // 8 == lax.broadcasted_iota(jnp.int32, (16, 128), 0)).astype(bf16)
    keep = lane[:8] % 8 == lax.broadcasted_iota(jnp.int32, (8, 128), 0)
    flat = []
    for ref in (labels_ref, mask_ref):
        wide = dot(ref[...].astype(f32).astype(bf16), spread)
        flat.append(jnp.sum(jnp.where(keep, wide, 0.0), axis=0, keepdims=True))
    row = lax.broadcasted_iota(jnp.int32, (16, 128), 0)
    out_ref[48:64, :] = jnp.where(row == 0, flat[0], jnp.where(row == 1, flat[1], 0.0)).astype(bf16)
    for copy in copies[6:]:
        copy.wait()


def weights_kernel(
    pair_ref, pair_bias_ref, head_ref, head_bias_ref, folded_ref, by_left_ref, by_right_ref, bias_ref, pair32_ref
):
    head_t = head_ref[...]
    pair32_ref[...] = pair_ref[...].astype(f32)
    head_twice = jnp.concatenate([head_t, head_t], axis=0)
    lane = lax.broadcasted_iota(jnp.int32, (128, 128), 1)
    for g in range(8):
        for q in range(4):
            at = (q * 8 + g) * 32
            by_left_ref[q * 32 : q * 32 + 32, g * 128 : g * 128 + 128] = pair_ref[at : at + 32, :]
            by_right_ref[q * 32 : q * 32 + 32, g * 128 : g * 128 + 128] = pair32_ref[
                pl.ds(q * 8 + g, 32, stride=32), :
            ].astype(bf16)
        product = dot(by_left_ref[:, g * 128 : g * 128 + 128], head_twice, NT)
        high = product.astype(bf16).astype(f32)
        folded_ref[g * 128 : g * 128 + 128, :] = jnp.where(lane < 64, high, product - high).astype(bf16)
    row = lax.broadcasted_iota(jnp.int32, (64, 64), 0)
    col = lax.broadcasted_iota(jnp.int32, (64, 64), 1)
    own_bias = jnp.sum(jnp.where(row == col, head_bias_ref[...], 0.0), axis=1, keepdims=True)
    bias_ref[...] = 2.0 * (jnp.sum(head_t.astype(f32) * pair_bias_ref[...], axis=1, keepdims=True) + own_bias)


def pairs_kernel(place_ref, scale_ref, *refs):
    pieces, refs = refs[:8], refs[8:]
    (
        folded_ref, bias_ref, head_ref, grad_ref, note_ref, groups_ref,
        turned_ref, left_ref, plain_ref, wide_ref, flat_ref, features_ref, half_ref, dhidden_ref,
    ) = refs
    place = place_ref[0]
    core = place // core_move % 2
    for n, piece in enumerate(pieces):
        for k in range(4):
            sender = place ^ (first_moves[k] ^ second_moves[n % 4] ^ n // 4 * core_move)
            at = k * 64
            turned_ref[pl.ds(pl.multiple_of(sender * 32, 32), 32), :] = piece[at : at + 32, :].astype(f32)
            plain_ref[pl.ds(pl.multiple_of(sender * 16, 16), 16), :] = piece[at + 32 : at + 48, :]
            flat_ref[pl.ds(pl.multiple_of(sender * 16, 16), 16), :] = piece[at + 48 : at + 64, :].astype(f32)
    for g in range(16):
        for p in range(2):
            groups_ref[p * 32 : p * 32 + 32, g * 128 : g * 128 + 128] = turned_ref[
                pl.ds(p * 16 + g, 32, stride=32), :
            ].astype(bf16)
    for q in range(2):
        for g in range(8):
            at = (q * 8 + g) * 32
            left_ref[at : at + 32, :] = turned_ref[pl.ds((core + q) % 2 * 16 + g, 32, stride=32), :].astype(bf16)
    source = lax.broadcasted_iota(jnp.int32, (128, 512), 0)
    target = lax.broadcasted_iota(jnp.int32, (128, 512), 1)
    copies = jnp.where(source == target // 128 * 32 + target % 32, 1.0 / 32.0, 0.0).astype(bf16)
    wide_ref[...] = dot(plain_ref[...], copies).astype(bf16)

    lane = lax.broadcasted_iota(jnp.int32, (32, 128), 1) // 32

    def outer_products(k, q):
        sides = []
        for d in (2 * k, 2 * k + 1):
            right = jnp.concatenate(
                [wide_ref[d * 16 : d * 16 + 16, (h * 2 + q) * 128 : (h * 2 + q + 1) * 128] for h in range(2)], axis=0
            )
            sides.append(
                jnp.concatenate([jnp.where(lane == c, right, jnp.zeros_like(right)) for c in range(4)], axis=0)
            )
        outer = dot(left_ref[q * 256 : q * 256 + 256, :], jnp.concatenate(sides, axis=1)).astype(bf16)
        for e in range(2):
            at = k * 128 + e * 64 + q * 32
            for g in range(8):
                features_ref[at : at + 32, g * 128 : g * 128 + 128] = outer[
                    g * 32 : g * 32 + 32, e * 128 : e * 128 + 128
                ]

    early = 1
    for k in range(16 + early):
        if k < 16:
            outer_products(k, 0)
            outer_products(k, 1)
        if k >= early:
            at = (k - early) * 128
            half_ref[at : at + 128, :] = dot(features_ref[at : at + 128, :], folded_ref[...])

    source = lax.broadcasted_iota(jnp.int32, (128, 512), 0)
    target = lax.broadcasted_iota(jnp.int32, (128, 512), 1)
    first = target // 128 * 4 + target // 32 % 4
    second = target % 32 * 2 + (core + first) % 2
    spread = (source == first * 8 + second % 8).astype(bf16)
    keep = second[0:32] // 8 == lax.broadcasted_iota(jnp.int32, (32, 512), 0) % 8

    def blocks(row):
        placed = dot(flat_ref[pl.ds(row, 32, stride=16), :].astype(bf16), spread)
        return jnp.sum(jnp.where(keep, placed, 0.0).reshape(4, 8, 512), axis=1)

    labels = blocks(0).astype(jnp.int32)
    mask = blocks(1)
    valid = jnp.sum(flat_ref[pl.ds(1, 32, stride=16), :], keepdims=True)
    factor = mask * (scale_ref[0] / valid)
    head2 = (2.0 * head_ref[...].astype(f32).T).astype(bf16)
    bins = lax.broadcasted_iota(jnp.int32, (64, 256), 0)
    loss = jnp.zeros((1, 256), f32)
    for k in range(8):
        tiles = []
        for d in (4 * k, 4 * k + 2):
            rows = [
                half_ref[pl.ds((core + q) % 2 * 32 + d + e, 32, stride=64), :] for e in range(2) for q in range(2)
            ]
            both = (half_ref[d * 64 : d * 64 + 128, :] + jnp.concatenate(rows, axis=0)).T
            tiles.append(both[0:64] + both[64:128])
        logits = jnp.concatenate(tiles, axis=1) + bias_ref[...]
        part = (slice(k // 2, k // 2 + 1), slice(k % 2 * 256, k % 2 * 256 + 256))
        shifted = logits - jnp.max(logits, axis=0, keepdims=True)
        exp_shift = jnp.exp(shifted)
        exp_total = jnp.sum(exp_shift, axis=0, keepdims=True)
        hit = bins == labels[part]
        picked = jnp.sum(jnp.where(hit, shifted, 0.0), axis=0, keepdims=True)
        loss = loss + mask[part] * (jnp.log(exp_total) - picked)
        here = factor[part]
        dlogits = exp_shift * (here / exp_total) - jnp.where(hit, here, 0.0)
        dhidden_ref[:, k * 256 : k * 256 + 256] = dot(head2, dlogits.astype(bf16)).astype(bf16)

    def of_device(d):
        columns = dhidden_ref[:, pl.ds(pl.multiple_of(d // 2 * 128, 128), 128)].astype(f32)
        return jnp.where(d % 2 == 0, columns[:, 0:64], columns[:, 64:128])

    note_ref[0:128, :] = jnp.concatenate([of_device(place ^ core_move), of_device(place)], axis=1)
    note_ref[128:136, :] = jnp.broadcast_to(jnp.sum(loss, axis=1, keepdims=True) / valid, (8, 128))

    for n in range(4):
        turned = dot(dhidden_ref[...], features_ref[:, n * 256 : n * 256 + 256]).T.astype(bf16)
        for g in range(2):
            for q in range(4):
                at = (q * 8 + n * 2 + g) * 32
                grad_ref[at : at + 32, :] = turned[g * 128 + q * 32 : g * 128 + q * 32 + 32]


def finish_kernel(
    place_ref, part_ref, other_part_ref, note_ref, other_ref, groups_ref, by_left_ref, by_right_ref,
    align_ref, gain_ref, proj_ref, loss_ref, align_grad_ref, weight_grad_ref,
):
    weight_grad_ref[...] = part_ref[...].astype(f32) + other_part_ref[...].astype(f32)
    core = place_ref[0] // core_move % 2
    loss_ref[...] = note_ref[128:129, 0:1] + other_ref[128:129, 0:1]
    mine, other = note_ref[0:128, 64:128], other_ref[0:128, 0:64]
    own = []
    for q in range(2):
        a, b = mine[:, q * 32 : q * 32 + 32], other[:, q * 32 : q * 32 + 32]
        odd = (core + q) % 2 == 1
        own.append(jnp.concatenate([jnp.where(odd, b, a), jnp.where(odd, a, b)], axis=1))
    sums = dot(jnp.concatenate(own, axis=0).astype(bf16), groups_ref[...]).astype(bf16)

    def contract(weights, base):
        q_rows = jnp.concatenate(
            [
                jnp.concatenate(
                    [sums[r * 128 : r * 128 + 128, (base + g) * 128 : (base + g + 1) * 128] for r in range(2)], axis=1
                )
                for g in range(8)
            ],
            axis=0,
        )
        full = dot(weights, q_rows)
        row = lax.broadcasted_iota(jnp.int32, (128, 256), 0) // 32
        col = lax.broadcasted_iota(jnp.int32, (128, 256), 1) // 32 % 4
        kept = jnp.where(row == col, full, 0.0)
        return kept[0:32] + kept[32:64] + kept[64:96] + kept[96:128]

    dleft = contract(by_right_ref[...], 8)
    dright = contract(by_left_ref[...], 0)
    dproj = jnp.concatenate([dleft, dright], axis=0).T * (1.0 / 32.0)
    proj = proj_ref[...]
    proj_twice = jnp.concatenate([proj, proj], axis=0)
    align = align_ref[...].astype(f32)
    for r in range(2):
        at = r * 128
        one = dproj[at : at + 32] + dproj[at + 32 : at + 64] + dproj[at + 64 : at + 96] + dproj[at + 96 : at + 128]
        high = one.astype(bf16)
        low = (one - high.astype(f32)).astype(bf16)
        dscaled = dot(jnp.concatenate([high, low], axis=1), proj_twice) * gain_ref[...]
        scaled, inverse = layer_norm(align[:, r, :])
        align_grad_ref[:, r, :] = inverse * (
            dscaled
            - jnp.mean(dscaled, axis=-1, keepdims=True)
            - scaled * jnp.mean(dscaled * scaled, axis=-1, keepdims=True)
        )


def spec(space=pltpu.VMEM):
    return pl.BlockSpec(memory_space=space)


def far(*arrays):
    return [pltpu.with_memory_space_constraint(a, pltpu.HBM) for a in arrays]


def held(*arrays):
    return [pltpu.VMEM(a.shape, a.dtype) for a in arrays]


def limit(mib):
    return pltpu.CompilerParams(vmem_limit_bytes=mib * 1024 * 1024)


def prepare(align, gain, proj_t, bias, labels_t, mask_t, *others):
    near = (align, gain, proj_t) + others
    local = (bias, labels_t, mask_t)
    return pl.pallas_call(
        prepare_kernel,
        out_shape=[jax.ShapeDtypeStruct((64, 128), bf16)] + [jax.ShapeDtypeStruct(a.shape, a.dtype) for a in near],
        in_specs=[spec(pltpu.HBM)] * 10,
        out_specs=[spec()] * 8,
        scratch_shapes=held(*local) + [pltpu.SemaphoreType.DMA((10,))],
        compiler_params=limit(2),
    )(*far(*near[:3], *local, *others))


def weights(*operands):
    return pl.pallas_call(
        weights_kernel,
        out_shape=(
            jax.ShapeDtypeStruct((1024, 128), bf16),
            jax.ShapeDtypeStruct((128, 1024), bf16),
            jax.ShapeDtypeStruct((128, 1024), bf16),
            jax.ShapeDtypeStruct((64, 1), f32),
        ),
        in_specs=[spec()] * 4,
        out_specs=[spec()] * 4,
        scratch_shapes=[pltpu.VMEM((1024, 128), f32)],
        compiler_params=limit(4),
    )(*operands)


def pairs(place, scale, pieces, *others):
    return pl.pallas_call(
        pairs_kernel,
        out_shape=(
            jax.ShapeDtypeStruct((1024, 128), bf16),
            jax.ShapeDtypeStruct((136, 128), f32),
            jax.ShapeDtypeStruct((64, 2048), bf16),
        ),
        in_specs=[spec(pltpu.SMEM)] * 2 + [spec()] * 11,
        out_specs=(spec(),) * 3,
        scratch_shapes=[
            pltpu.VMEM((1024, 128), f32),
            pltpu.VMEM((512, 128), bf16),
            pltpu.VMEM((512, 128), bf16),
            pltpu.VMEM((512, 512), bf16),
            pltpu.VMEM((512, 128), f32),
            pltpu.VMEM((2048, 1024), bf16),
            pltpu.VMEM((2048, 128), f32),
            pltpu.VMEM((128, 2048), bf16),
        ],
        compiler_params=limit(20),
    )(place, scale, *pieces, *others)


def finish(place, *others):
    return pl.pallas_call(
        finish_kernel,
        out_shape=(
            jax.ShapeDtypeStruct((1, 1), f32),
            jax.ShapeDtypeStruct((32, 2, 256), f32),
            jax.ShapeDtypeStruct((1024, 128), f32),
        ),
        in_specs=[spec(pltpu.SMEM)] + [spec()] * 10,
        out_specs=(spec(),) * 3,
        compiler_params=limit(8),
    )(place, *others)


def join_kernel(*refs):
    for n, part in enumerate(refs[:4]):
        refs[4][n * 64 : n * 64 + 64, :] = part[...]


def join(parts):
    return pl.pallas_call(
        join_kernel,
        out_shape=jax.ShapeDtypeStruct((256, 128), bf16),
        in_specs=[spec()] * 4,
        out_specs=spec(),
        compiler_params=limit(2),
    )(*parts)


first_moves = (0, 2, 4, 6)
second_moves = (0, 1, 16, 17)
core_move = 8


def swap(block, move):
    return lax.ppermute(block, ("row", "col"), [(d, d ^ move) for d in range(32)])


def gather(message):
    line = join([message] + [swap(message, move) for move in first_moves[1:]])
    plane = [line] + [swap(line, move) for move in second_moves[1:]]
    return plane + [swap(block, core_move) for block in plane]


def local_whole(
    alignment, norm_gain, norm_bias, proj_weight, pair_weight, pair_bias, head_weight, head_bias,
    labels, pair_mask, loss_scale,
):
    message, align, gain, proj_t, pair, pair_bias, head_t, head_bias = prepare(
        alignment, norm_gain.reshape(1, 256), proj_weight.T, norm_bias.reshape(1, 256), labels.T, pair_mask.T,
        pair_weight, pair_bias.reshape(1, 128), head_weight.T, head_bias.reshape(1, 64),
    )
    folded, by_left, by_right, bias = weights(pair, pair_bias, head_t, head_bias)
    pieces = gather(message)
    place = lax.axis_index(("row", "col")).astype(jnp.int32).reshape(1)
    part, note, groups = pairs(place, loss_scale.reshape(1), pieces, folded, bias, head_t)
    loss, align_grad, weight_grad = finish(
        place, part, swap(part, core_move), note, swap(note, core_move), groups, by_left, by_right,
        align, gain, proj_t,
    )
    return (loss.reshape(()), align_grad, weight_grad)


def solution(mesh):
    in_specs = (
        P(None, ("row", "col"), None),
        P(),
        P(),
        P(),
        P(),
        P(),
        P(),
        P(),
        P("row", "col"),
        P("row", "col"),
        P(),
    )
    out_specs = (P(), P(None, ("row", "col"), None), P())
    def whole(alignment, *others):
        sequences, residues, channels = alignment.shape
        small = (
            (sequences, residues, channels) == (32, 64, 256)
            and tuple(mesh.shape.values()) == (4, 8)
            and others[2].shape[1] == 64
            and others[3].shape == (1024, 128)
            and others[5].shape == (128, 64)
        )
        return jax.shard_map(
            local_whole if small else local, mesh=mesh, in_specs=in_specs, out_specs=out_specs, check_vma=False
        )(alignment, *others)

    return whole
```

```python
import functools

import jax
import jax.numpy as jnp
from jax import lax
from jax.experimental import pallas as pl
from jax.experimental.pallas import tpu as pltpu
from jax.sharding import PartitionSpec as P

norm_eps = 1e-05
highest = lax.Precision.HIGHEST


def from_root(value, axis, source):
    kept = jnp.where(lax.axis_index(axis) == source, value, 0).astype(value.dtype)
    return lax.psum(kept, axis)


def normalize(alignment, norm_gain, norm_bias):
    values = alignment.astype(jnp.float32)
    centered = values - jnp.mean(values, axis=-1, keepdims=True)
    inverse = lax.rsqrt(jnp.mean(centered * centered, axis=-1, keepdims=True) + norm_eps)
    scaled = centered * inverse
    normed = (scaled * norm_gain + norm_bias).astype(jnp.bfloat16)
    return (scaled, inverse, normed)


def pair_features(left_proj, right_proj, mirrored):
    if mirrored:
        outer = jnp.einsum(
            "sid,sjc->ijcd", left_proj, right_proj, preferred_element_type=jnp.float32
        )
    else:
        outer = jnp.einsum(
            "sic,sjd->ijcd", left_proj, right_proj, preferred_element_type=jnp.float32
        )
    outer = outer * (1.0 / left_proj.shape[0])
    return outer.astype(jnp.bfloat16).reshape(-1, outer.shape[2] * outer.shape[3])


def local(
    alignment,
    norm_gain,
    norm_bias,
    proj_weight,
    pair_weight,
    pair_bias,
    head_weight,
    head_bias,
    labels,
    pair_mask,
    loss_scale,
):
    per_row = lax.axis_size("col") // lax.axis_size("row")
    col_place = lax.axis_index("col")
    row_place = lax.axis_index("row")
    sequences = alignment.shape[0]
    outer_width = proj_weight.shape[1] // 2
    bin_count = head_weight.shape[1]
    scaled, inverse, normed = normalize(alignment, norm_gain, norm_bias)
    projected = jnp.einsum(
        "src,cp->srp", normed, proj_weight, preferred_element_type=jnp.float32
    ).astype(jnp.bfloat16)
    mask_values = pair_mask.astype(jnp.float32)
    valid_pairs = lax.psum(jnp.sum(mask_values), ("row", "col"))
    row_proj = lax.all_gather(projected, "col", axis=1, tiled=True)
    row_span = row_proj.shape[1]
    col_span = row_span // per_row
    offset = col_place % per_row * col_span
    own_slice = lax.dynamic_slice_in_dim(row_proj, offset, col_span, 1)
    col_proj = from_root(own_slice, "row", col_place // per_row)
    pair32 = pair_weight.astype(jnp.float32)
    head32 = head_weight.astype(jnp.float32)
    weight_shape = pair32.shape
    grad_width = 2 * outer_width
    block_rows = min(row_span, max(1, 512 // col_span))
    num_blocks = row_span // block_rows
    grad_factor = loss_scale / valid_pairs
    inv_seqs = 1.0 / sequences
    bins_iota = lax.broadcasted_iota(jnp.int32, (block_rows * col_span, bin_count), 1)

    def pair_head(features):
        hidden = jnp.dot(features, pair_weight, preferred_element_type=jnp.float32) + pair_bias
        return jnp.dot(hidden, head32, precision=highest) + head_bias

    def tile_back(features, dhalf, left_proj, right_proj, mirrored):
        dhidden = jnp.dot(dhalf, head_weight.T, preferred_element_type=jnp.float32)
        dfeatures = jnp.dot(dhidden, pair32.T, precision=highest)
        weight_term = jnp.dot(features.astype(jnp.float32).T, dhidden, precision=highest)
        dfeatures = dfeatures.astype(jnp.bfloat16).reshape(
            left_proj.shape[1], right_proj.shape[1], outer_width, outer_width
        )
        if mirrored:
            grad_left = jnp.einsum(
                "ijcd,sjc->sid", dfeatures, right_proj, preferred_element_type=jnp.float32
            )
            grad_right = jnp.einsum(
                "ijcd,sid->sjc", dfeatures, left_proj, preferred_element_type=jnp.float32
            )
        else:
            grad_left = jnp.einsum(
                "ijcd,sjd->sic", dfeatures, right_proj, preferred_element_type=jnp.float32
            )
            grad_right = jnp.einsum(
                "ijcd,sic->sjd", dfeatures, left_proj, preferred_element_type=jnp.float32
            )
        return (grad_left * inv_seqs, grad_right * inv_seqs, weight_term)

    def block_step(block_index, carry):
        loss_sum, weight_sum, row_grad, col_grad = carry
        first_row = block_index * block_rows
        rows_here = lax.dynamic_slice_in_dim(row_proj, first_row, block_rows, 1)
        left_own = rows_here[:, :, :outer_width]
        left_mirror = rows_here[:, :, outer_width:]
        right_own = col_proj[:, :, outer_width:]
        right_mirror = col_proj[:, :, :outer_width]
        own_features = pair_features(left_own, right_own, False)
        mirror_features = pair_features(left_mirror, right_mirror, True)
        logits = pair_head(own_features) + pair_head(mirror_features)
        labels_here = lax.dynamic_slice_in_dim(labels, first_row, block_rows, 0).reshape(-1)
        mask_here = lax.dynamic_slice_in_dim(mask_values, first_row, block_rows, 0).reshape(-1)
        row_top = jnp.max(logits, axis=-1, keepdims=True)
        shifted = logits - row_top
        exp_shift = jnp.exp(shifted)
        exp_total = jnp.sum(exp_shift, axis=-1, keepdims=True)
        target = bins_iota == labels_here[:, None]
        picked = jnp.sum(jnp.where(target, shifted, 0.0), axis=-1)
        loss_sum = loss_sum + jnp.sum(mask_here * (jnp.log(exp_total[:, 0]) - picked))
        dlogits = (
            (exp_shift / exp_total - target.astype(jnp.float32))
            * (mask_here * grad_factor)[:, None]
        ).astype(jnp.bfloat16)
        grad_left, grad_right, weight_term = tile_back(
            own_features, dlogits, left_own, right_own, False
        )
        mirror_left, mirror_right, mirror_term = tile_back(
            mirror_features, dlogits, left_mirror, right_mirror, True
        )
        row_part = jnp.concatenate([grad_left, mirror_left], axis=-1)
        col_part = jnp.concatenate([mirror_right, grad_right], axis=-1)
        weight_term = weight_term + mirror_term
        row_grad = lax.dynamic_update_slice_in_dim(row_grad, row_part, first_row, 1)
        return (loss_sum, weight_sum + weight_term, row_grad, col_grad + col_part)

    initial = (
        jnp.zeros((), jnp.float32),
        jnp.zeros(weight_shape, jnp.float32),
        jnp.zeros((sequences, row_span, grad_width), jnp.float32),
        jnp.zeros((sequences, col_span, grad_width), jnp.float32),
    )
    loss_sum, weight_sum, row_grad, col_grad = lax.fori_loop(0, num_blocks, block_step, initial)
    holder = col_place // per_row == row_place
    col_sum = lax.psum(col_grad.astype(jnp.bfloat16), "row").astype(jnp.float32)
    placed = lax.dynamic_update_slice_in_dim(jnp.zeros_like(row_grad), col_sum, offset, 1)
    contribution = row_grad + jnp.where(holder, placed, 0.0)
    own_grad = lax.psum_scatter(contribution, "col", scatter_dimension=1, tiled=True)
    dnormed = jnp.einsum(
        "srp,cp->src", own_grad, proj_weight.astype(jnp.float32), precision=highest
    )
    dscaled = dnormed * norm_gain
    alignment_grad = inverse * (
        dscaled
        - jnp.mean(dscaled, axis=-1, keepdims=True)
        - scaled * jnp.mean(dscaled * scaled, axis=-1, keepdims=True)
    )
    loss_total, pair_weight_grad = lax.psum((loss_sum, weight_sum), ("row", "col"))
    return (loss_total / valid_pairs, alignment_grad, pair_weight_grad)


f32 = jnp.float32
bf16 = jnp.bfloat16
NN = (((1,), (0,)), ((), ()))
NT = (((1,), (1,)), ((), ()))


def dot(a, b, dims=NN):
    return lax.dot_general(a, b, dims, preferred_element_type=f32)


def layer_norm(x):
    centered = x - jnp.mean(x, axis=-1, keepdims=True)
    inverse = lax.rsqrt(jnp.mean(centered * centered, axis=-1, keepdims=True) + norm_eps)
    return centered * inverse, inverse


def fetch(sources, targets, sems):
    copies = [
        pltpu.make_async_copy(source, target, sems.at[n])
        for n, (source, target) in enumerate(zip(sources, targets, strict=True))
    ]
    for copy in copies:
        copy.start()
    return copies


def prepare_kernel(*refs):
    sources, out_ref, near, scratch, sems = refs[:10], refs[10], refs[11:18], refs[18:21], refs[21]
    align_ref, gain_ref, weight_ref = near[:3]
    bias_ref, labels_ref, mask_ref = scratch
    copies = fetch(sources, near[:3] + scratch + near[3:], sems)
    for copy in copies[:6]:
        copy.wait()
    align = align_ref[...].astype(f32)
    weight = weight_ref[...]
    plain = []
    for r in range(2):
        scaled, _ = layer_norm(align[:, r, :])
        normed = (scaled * gain_ref[...] + bias_ref[...]).astype(bf16)
        turned = dot(weight, normed, NT)
        rows = [
            jnp.concatenate([turned[h * 32 + q * 8 : h * 32 + q * 8 + 8] for q in range(4)], axis=1)
            for h in range(2)
        ]
        out_ref[r * 16 : r * 16 + 16, :] = jnp.concatenate(rows, axis=0).astype(bf16)
        plain.append(dot(normed, weight[32:64], NT))
    out_ref[32:48, :] = jnp.concatenate(
        [plain[r][h * 16 : h * 16 + 16] for h in range(2) for r in range(2)], axis=1
    ).astype(bf16)
    lane = lax.broadcasted_iota(jnp.int32, (16, 128), 1)
    spread = (lane // 8 == lax.broadcasted_iota(jnp.int32, (16, 128), 0)).astype(bf16)
    keep = lane[:8] % 8 == lax.broadcasted_iota(jnp.int32, (8, 128), 0)
    flat = []
    for ref in (labels_ref, mask_ref):
        wide = dot(ref[...].astype(f32).astype(bf16), spread)
        flat.append(jnp.sum(jnp.where(keep, wide, 0.0), axis=0, keepdims=True))
    row = lax.broadcasted_iota(jnp.int32, (16, 128), 0)
    out_ref[48:64, :] = jnp.where(row == 0, flat[0], jnp.where(row == 1, flat[1], 0.0)).astype(bf16)
    for copy in copies[6:]:
        copy.wait()


def weights_kernel(
    pair_ref, pair_bias_ref, head_ref, head_bias_ref, folded_ref, by_left_ref, by_right_ref, bias_ref, pair32_ref
):
    head_t = head_ref[...]
    pair32_ref[...] = pair_ref[...].astype(f32)
    head_twice = jnp.concatenate([head_t, head_t], axis=0)
    lane = lax.broadcasted_iota(jnp.int32, (128, 128), 1)
    for g in range(8):
        for q in range(4):
            at = (q * 8 + g) * 32
            by_left_ref[q * 32 : q * 32 + 32, g * 128 : g * 128 + 128] = pair_ref[at : at + 32, :]
            by_right_ref[q * 32 : q * 32 + 32, g * 128 : g * 128 + 128] = pair32_ref[
                pl.ds(q * 8 + g, 32, stride=32), :
            ].astype(bf16)
        product = dot(by_left_ref[:, g * 128 : g * 128 + 128], head_twice, NT)
        high = product.astype(bf16).astype(f32)
        folded_ref[g * 128 : g * 128 + 128, :] = jnp.where(lane < 64, high, product - high).astype(bf16)
    row = lax.broadcasted_iota(jnp.int32, (64, 64), 0)
    col = lax.broadcasted_iota(jnp.int32, (64, 64), 1)
    own_bias = jnp.sum(jnp.where(row == col, head_bias_ref[...], 0.0), axis=1, keepdims=True)
    bias_ref[...] = 2.0 * (jnp.sum(head_t.astype(f32) * pair_bias_ref[...], axis=1, keepdims=True) + own_bias)


def pairs_kernel(place_ref, scale_ref, *refs):
    pieces, refs = refs[:8], refs[8:]
    (
        folded_ref, bias_ref, head_ref, grad_ref, note_ref, groups_ref,
        turned_ref, left_ref, plain_ref, wide_ref, flat_ref, features_ref, half_ref, dhidden_ref,
    ) = refs
    place = place_ref[0]
    core = place // core_move % 2
    for n, piece in enumerate(pieces):
        for k in range(4):
            sender = place ^ (first_moves[k] ^ second_moves[n % 4] ^ n // 4 * core_move)
            at = k * 64
            turned = piece[at : at + 32, :].astype(f32)
            for r in range(2):
                turned_ref[pl.ds(r * 32 + sender, 16, stride=64), :] = turned[r * 16 : r * 16 + 16]
            plain_ref[pl.ds(pl.multiple_of(sender * 16, 16), 16), :] = piece[at + 32 : at + 48, :]
            flat = piece[at + 48 : at + 64, :].astype(f32)
            flat_ref[pl.ds(sender, 1), :] = flat[0:1]
            flat_ref[pl.ds(sender + 32, 1), :] = flat[1:2]
    for g in range(16):
        groups_ref[:, g * 128 : g * 128 + 128] = turned_ref[g * 64 : g * 64 + 64, :].astype(bf16)
    for q in range(2):
        for g in range(8):
            at = (q * 8 + g) * 32
            side = pl.multiple_of(g * 64 + (core + q) % 2 * 32, 32)
            left_ref[at : at + 32, :] = turned_ref[pl.ds(side, 32), :].astype(bf16)
    source = lax.broadcasted_iota(jnp.int32, (128, 512), 0)
    target = lax.broadcasted_iota(jnp.int32, (128, 512), 1)
    copies = jnp.where(source == target // 128 * 32 + target % 32, 1.0 / 32.0, 0.0).astype(bf16)
    wide_ref[...] = dot(plain_ref[...], copies).astype(bf16)

    lane = lax.broadcasted_iota(jnp.int32, (32, 128), 1) // 32

    def outer_products(k, q):
        sides = []
        for d in (2 * k, 2 * k + 1):
            right = jnp.concatenate(
                [wide_ref[d * 16 : d * 16 + 16, (h * 2 + q) * 128 : (h * 2 + q + 1) * 128] for h in range(2)], axis=0
            )
            sides.append(
                jnp.concatenate([jnp.where(lane == c, right, jnp.zeros_like(right)) for c in range(4)], axis=0)
            )
        outer = dot(left_ref[q * 256 : q * 256 + 256, :], jnp.concatenate(sides, axis=1)).astype(bf16)
        for e in range(2):
            at = k * 128 + e * 64 + q * 32
            for g in range(8):
                features_ref[at : at + 32, g * 128 : g * 128 + 128] = outer[
                    g * 32 : g * 32 + 32, e * 128 : e * 128 + 128
                ]

    early = 1
    for k in range(16 + early):
        if k < 16:
            outer_products(k, 0)
            outer_products(k, 1)
        if k >= early:
            at = (k - early) * 128
            half_ref[at : at + 128, :] = dot(features_ref[at : at + 128, :], folded_ref[...])

    source = lax.broadcasted_iota(jnp.int32, (128, 512), 0)
    target = lax.broadcasted_iota(jnp.int32, (128, 512), 1)
    first = target // 128 * 4 + target // 32 % 4
    second = target % 32 * 2 + (core + first) % 2
    spread = (source == first * 8 + second % 8).astype(bf16)
    keep = second[0:32] // 8 == lax.broadcasted_iota(jnp.int32, (32, 512), 0) % 8

    def blocks(row):
        placed = dot(flat_ref[row * 32 : row * 32 + 32, :].astype(bf16), spread)
        return jnp.sum(jnp.where(keep, placed, 0.0).reshape(4, 8, 512), axis=1)

    labels = blocks(0).astype(jnp.int32)
    mask = blocks(1)
    valid = jnp.sum(flat_ref[32:64, :], keepdims=True)
    factor = mask * (scale_ref[0] / valid)
    head2 = (2.0 * head_ref[...].astype(f32).T).astype(bf16)
    bins = lax.broadcasted_iota(jnp.int32, (64, 256), 0)
    loss = jnp.zeros((1, 256), f32)
    for k in range(8):
        tiles = []
        for d in (4 * k, 4 * k + 2):
            rows = [
                half_ref[pl.ds((core + q) % 2 * 32 + d + e, 32, stride=64), :] for e in range(2) for q in range(2)
            ]
            both = (half_ref[d * 64 : d * 64 + 128, :] + jnp.concatenate(rows, axis=0)).T
            tiles.append(both[0:64] + both[64:128])
        logits = jnp.concatenate(tiles, axis=1) + bias_ref[...]
        part = (slice(k // 2, k // 2 + 1), slice(k % 2 * 256, k % 2 * 256 + 256))
        shifted = logits - jnp.max(logits, axis=0, keepdims=True)
        exp_shift = jnp.exp(shifted)
        exp_total = jnp.sum(exp_shift, axis=0, keepdims=True)
        hit = bins == labels[part]
        picked = jnp.sum(jnp.where(hit, shifted, 0.0), axis=0, keepdims=True)
        loss = loss + mask[part] * (jnp.log(exp_total) - picked)
        here = factor[part]
        dlogits = exp_shift * (here / exp_total) - jnp.where(hit, here, 0.0)
        dhidden_ref[:, k * 256 : k * 256 + 256] = dot(head2, dlogits.astype(bf16)).astype(bf16)

    def of_device(d):
        columns = dhidden_ref[:, pl.ds(pl.multiple_of(d // 2 * 128, 128), 128)].astype(f32)
        return jnp.where(d % 2 == 0, columns[:, 0:64], columns[:, 64:128])

    note_ref[0:128, :] = jnp.concatenate([of_device(place ^ core_move), of_device(place)], axis=1)
    note_ref[128:136, :] = jnp.broadcast_to(jnp.sum(loss, axis=1, keepdims=True) / valid, (8, 128))

    for n in range(4):
        turned = dot(dhidden_ref[...], features_ref[:, n * 256 : n * 256 + 256]).T.astype(bf16)
        for g in range(2):
            for q in range(4):
                at = (q * 8 + n * 2 + g) * 32
                grad_ref[at : at + 32, :] = turned[g * 128 + q * 32 : g * 128 + q * 32 + 32]


def finish_kernel(
    place_ref, part_ref, other_part_ref, note_ref, other_ref, groups_ref, by_left_ref, by_right_ref,
    align_ref, gain_ref, proj_ref, loss_ref, align_grad_ref, weight_grad_ref,
):
    weight_grad_ref[...] = part_ref[...].astype(f32) + other_part_ref[...].astype(f32)
    core = place_ref[0] // core_move % 2
    loss_ref[...] = note_ref[128:129, 0:1] + other_ref[128:129, 0:1]
    mine, other = note_ref[0:128, 64:128], other_ref[0:128, 0:64]
    own = []
    for q in range(2):
        a, b = mine[:, q * 32 : q * 32 + 32], other[:, q * 32 : q * 32 + 32]
        odd = (core + q) % 2 == 1
        own.append(jnp.concatenate([jnp.where(odd, b, a), jnp.where(odd, a, b)], axis=1))
    sums = dot(jnp.concatenate(own, axis=0).astype(bf16), groups_ref[...]).astype(bf16)

    def contract(weights, base):
        q_rows = jnp.concatenate(
            [
                jnp.concatenate(
                    [sums[r * 128 : r * 128 + 128, (base + g) * 128 : (base + g + 1) * 128] for r in range(2)], axis=1
                )
                for g in range(8)
            ],
            axis=0,
        )
        full = dot(weights, q_rows)
        row = lax.broadcasted_iota(jnp.int32, (128, 256), 0) // 32
        col = lax.broadcasted_iota(jnp.int32, (128, 256), 1) // 32 % 4
        kept = jnp.where(row == col, full, 0.0)
        return kept[0:32] + kept[32:64] + kept[64:96] + kept[96:128]

    dleft = contract(by_right_ref[...], 8)
    dright = contract(by_left_ref[...], 0)
    dproj = jnp.concatenate([dleft, dright], axis=0).T * (1.0 / 32.0)
    proj = proj_ref[...]
    proj_twice = jnp.concatenate([proj, proj], axis=0)
    align = align_ref[...].astype(f32)
    for r in range(2):
        at = r * 128
        one = dproj[at : at + 32] + dproj[at + 32 : at + 64] + dproj[at + 64 : at + 96] + dproj[at + 96 : at + 128]
        high = one.astype(bf16)
        low = (one - high.astype(f32)).astype(bf16)
        dscaled = dot(jnp.concatenate([high, low], axis=1), proj_twice) * gain_ref[...]
        scaled, inverse = layer_norm(align[:, r, :])
        align_grad_ref[:, r, :] = inverse * (
            dscaled
            - jnp.mean(dscaled, axis=-1, keepdims=True)
            - scaled * jnp.mean(dscaled * scaled, axis=-1, keepdims=True)
        )


def spec(space=pltpu.VMEM):
    return pl.BlockSpec(memory_space=space)


def far(*arrays):
    return [pltpu.with_memory_space_constraint(a, pltpu.HBM) for a in arrays]


def held(*arrays):
    return [pltpu.VMEM(a.shape, a.dtype) for a in arrays]


def limit(mib):
    return pltpu.CompilerParams(vmem_limit_bytes=mib * 1024 * 1024)


def prepare(align, gain, proj_t, bias, labels_t, mask_t, *others):
    near = (align, gain, proj_t) + others
    local = (bias, labels_t, mask_t)
    return pl.pallas_call(
        prepare_kernel,
        out_shape=[jax.ShapeDtypeStruct((64, 128), bf16)] + [jax.ShapeDtypeStruct(a.shape, a.dtype) for a in near],
        in_specs=[spec(pltpu.HBM)] * 10,
        out_specs=[spec()] * 8,
        scratch_shapes=held(*local) + [pltpu.SemaphoreType.DMA((10,))],
        compiler_params=limit(2),
    )(*far(*near[:3], *local, *others))


def weights(*operands):
    return pl.pallas_call(
        weights_kernel,
        out_shape=(
            jax.ShapeDtypeStruct((1024, 128), bf16),
            jax.ShapeDtypeStruct((128, 1024), bf16),
            jax.ShapeDtypeStruct((128, 1024), bf16),
            jax.ShapeDtypeStruct((64, 1), f32),
        ),
        in_specs=[spec()] * 4,
        out_specs=[spec()] * 4,
        scratch_shapes=[pltpu.VMEM((1024, 128), f32)],
        compiler_params=limit(4),
    )(*operands)


def pairs(place, scale, pieces, *others):
    return pl.pallas_call(
        pairs_kernel,
        out_shape=(
            jax.ShapeDtypeStruct((1024, 128), bf16),
            jax.ShapeDtypeStruct((136, 128), f32),
            jax.ShapeDtypeStruct((64, 2048), bf16),
        ),
        in_specs=[spec(pltpu.SMEM)] * 2 + [spec()] * 11,
        out_specs=(spec(),) * 3,
        scratch_shapes=[
            pltpu.VMEM((1024, 128), f32),
            pltpu.VMEM((512, 128), bf16),
            pltpu.VMEM((512, 128), bf16),
            pltpu.VMEM((512, 512), bf16),
            pltpu.VMEM((64, 128), f32),
            pltpu.VMEM((2048, 1024), bf16),
            pltpu.VMEM((2048, 128), f32),
            pltpu.VMEM((128, 2048), bf16),
        ],
        compiler_params=limit(20),
    )(place, scale, *pieces, *others)


def finish(place, *others):
    return pl.pallas_call(
        finish_kernel,
        out_shape=(
            jax.ShapeDtypeStruct((1, 1), f32),
            jax.ShapeDtypeStruct((32, 2, 256), f32),
            jax.ShapeDtypeStruct((1024, 128), f32),
        ),
        in_specs=[spec(pltpu.SMEM)] + [spec()] * 10,
        out_specs=(spec(),) * 3,
        compiler_params=limit(8),
    )(place, *others)


def join_kernel(after_ref, *refs):
    del after_ref
    for n, part in enumerate(refs[:4]):
        refs[4][n * 64 : n * 64 + 64, :] = part[...]


def join(parts, after):
    return pl.pallas_call(
        join_kernel,
        out_shape=jax.ShapeDtypeStruct((256, 128), bf16),
        in_specs=[spec(pl.ANY)] + [spec()] * 4,
        out_specs=spec(),
        compiler_params=limit(2),
    )(after, *parts)


first_moves = (0, 2, 4, 6)
second_moves = (0, 1, 16, 17)
core_move = 8


def swap(block, move):
    return lax.ppermute(block, ("row", "col"), [(d, d ^ move) for d in range(32)])


def gather(message, after):
    line = join([message] + [swap(message, move) for move in first_moves[1:]], after)
    plane = [line] + [swap(line, move) for move in second_moves[1:]]
    return plane + [swap(block, core_move) for block in plane]


def local_whole(
    alignment, norm_gain, norm_bias, proj_weight, pair_weight, pair_bias, head_weight, head_bias,
    labels, pair_mask, loss_scale,
):
    message, align, gain, proj_t, pair, pair_bias, head_t, head_bias = prepare(
        alignment, norm_gain.reshape(1, 256), proj_weight.T, norm_bias.reshape(1, 256), labels.T, pair_mask.T,
        pair_weight, pair_bias.reshape(1, 128), head_weight.T, head_bias.reshape(1, 64),
    )
    folded, by_left, by_right, bias = weights(pair, pair_bias, head_t, head_bias)
    pieces = gather(message, bias)
    place = lax.axis_index(("row", "col")).astype(jnp.int32).reshape(1)
    part, note, groups = pairs(place, loss_scale.reshape(1), pieces, folded, bias, head_t)
    loss, align_grad, weight_grad = finish(
        place, part, swap(part, core_move), note, swap(note, core_move), groups, by_left, by_right,
        align, gain, proj_t,
    )
    return (loss.reshape(()), align_grad, weight_grad)


def solution(mesh):
    in_specs = (
        P(None, ("row", "col"), None),
        P(),
        P(),
        P(),
        P(),
        P(),
        P(),
        P(),
        P("row", "col"),
        P("row", "col"),
        P(),
    )
    out_specs = (P(), P(None, ("row", "col"), None), P())
    def whole(alignment, *others):
        sequences, residues, channels = alignment.shape
        small = (
            (sequences, residues, channels) == (32, 64, 256)
            and tuple(mesh.shape.values()) == (4, 8)
            and others[2].shape[1] == 64
            and others[3].shape == (1024, 128)
            and others[5].shape == (128, 64)
        )
        return jax.shard_map(
            local_whole if small else local, mesh=mesh, in_specs=in_specs, out_specs=out_specs, check_vma=False
        )(alignment, *others)

    return whole
```
